32 devices in a mesh: group: 2 (over y), row: 16 (over z, x, core).
Axes of the slice: x: 2, y: 2, z: 4, core: 2. Of those that a mesh axis runs over, the one named last changes fastest.
Arguments:
- image: bfloat16 [128, 256, 256], P(('group', 'row')), parts along dimension 0, may hold values from -6 to 6
- tissue: int32 [32, 2], P(('group', 'row')), parts along dimension 0, may hold values from 0 to 1, as said below
- kernel: float32 [7, 7, 256], replicated, may hold values from -0.875 to 0.875
- ln_gain: float32 [256], replicated, may hold values from 0.5 to 1.5
- w_in: bfloat16 [256, 1024], replicated, may hold values from -0.375 to 0.375
- w_out: bfloat16 [1024, 256], replicated, may hold values from -0.1875 to 0.1875
- layer_scale: float32 [256], replicated, may hold values from 0.5 to 1.5
- cotangent: bfloat16 [128, 256, 256], P(('group', 'row')), parts along dimension 0, may hold values from -6 to 6
Outputs:
- block_out: bfloat16 [128, 256, 256], P(('group', 'row')), parts along dimension 0
- grad_image: bfloat16 [128, 256, 256], P(('group', 'row')), parts along dimension 0
- grad_w_in: float32 [512, 1024], P(('group', 'row')), parts along dimension 0
- grad_w_out: float32 [2048, 256], P(('group', 'row')), parts along dimension 0
- small_grads: float32 [102, 256], P('group'), parts along dimension 0
The draws below stay inside these ranges and needn't reach their ends.
There are 2 independent parts, one for each index of `group`. The reference program is written for one: setup_inputs(seed, part) draws one part's arguments, and reference() takes and returns one part's arrays. A program takes and returns all parts, laid end to end along the dimension named above; an argument that names none is the same for every part. Nothing has to cross between parts.
Inputs may be any that keep to these rules, and one draw needn't show every extreme that they name: 1 marks a tile of 4 x 128 positions that holds tissue, 0 one without. Among the 2 tiles of the 4 rows of one device, at least one is 0 and at least one is 1.
All inputs are finite; a program needn't handle non-finite values.
Results may differ from the reference program's by a relative error of at most 0.0063.
Values may be sent and summed in bfloat16 or wider, within the bound.
A program may use at most 64 MiB of HBM per device.

```python
import jax
import jax.numpy as jnp
from jax import lax

C = 256
FF = 1024
KERNEL = 7
TILE_ROWS = 4
TILE_COLS = 128
ROWS_DEV = 4
COLS = 256
ROWS = 64


def draw_tissue(key, part):
    tile_rows = ROWS // TILE_ROWS
    tile_cols = COLS // TILE_COLS
    device_blocks = ROWS // ROWS_DEV
    tiles_dev = ROWS_DEV // TILE_ROWS * tile_cols
    emptied = max(1, tiles_dev // 4)
    ballots = jax.random.randint(jax.random.fold_in(key, 11), (tile_rows, tile_cols), 0, 100)
    ceiling = 25 + jnp.arange(tile_rows, dtype=jnp.int32) * 45 // tile_rows
    marked = (ballots < ceiling[:, None]).astype(jnp.int32)
    scores = jax.random.randint(jax.random.fold_in(key, 23), (device_blocks, tiles_dev), 0, 1048576)
    scores = scores * tiles_dev + jnp.arange(tiles_dev, dtype=jnp.int32)[None, :]
    order = jnp.argsort(scores, axis=1)
    ranks = jnp.argsort(order, axis=1).astype(jnp.int32)
    keep = (ranks >= emptied).astype(jnp.int32)
    forced = (ranks == tiles_dev - 1).astype(jnp.int32)
    marked = jnp.maximum(marked.reshape(device_blocks, tiles_dev) * keep, forced)
    return marked.reshape(tile_rows, tile_cols)


def shard_levels(own_key, dims, cuts, smallest, largest):
    def one(dim, parts):
        heights = jax.random.uniform(jax.random.fold_in(jax.random.fold_in(own_key, 6), dim), (parts,), jnp.float32, smallest / len(cuts), largest / len(cuts))
        return jnp.repeat(jnp.exp(heights), dims[dim] // parts).reshape((-1,) + (1,) * (len(dims) - dim - 1))

    level = one(*cuts[0])
    for cut in cuts[1:]:
        level = level * one(*cut)
    return level


def bell_draw(rng, shape, scale, bound, shards=(), kind=jnp.bfloat16):
    drawn = jax.random.normal(rng, shape, jnp.float32) * scale
    if len(shards) > 0:
        drawn = shard_levels(rng, shape, shards, -0.22, 0.18) * drawn
    return jnp.clip(drawn, min=-bound, max=bound).astype(kind)


def setup_inputs(seed: int = 0, part: int = 0) -> dict:
    streams_of = jax.random.split(jax.random.key(seed), 9)
    own_keys = jax.random.split(jax.random.fold_in(streams_of[8], part), 9)
    image = bell_draw(own_keys[0], (ROWS, COLS, C), 1.0, 6.0, ((0, 16),))
    tissue = draw_tissue(jax.random.fold_in(jax.random.fold_in(streams_of[8], part), 71), part)
    kernel = bell_draw(streams_of[2], (KERNEL, KERNEL, C), (KERNEL * KERNEL) ** -0.5, 0.875, (), jnp.float32)
    ln_gain = jnp.clip(jax.random.uniform(streams_of[3], (C,), jnp.float32, 0.5, 1.5), 0.5, 1.5)
    w_in = bell_draw(streams_of[4], (C, FF), C ** -0.5, 0.375)
    w_out = bell_draw(streams_of[5], (FF, C), FF ** -0.5, 0.1875)
    layer_scale = jnp.clip(jax.random.uniform(streams_of[6], (C,), jnp.float32, 0.5, 1.5), 0.5, 1.5)
    cotangent = bell_draw(own_keys[7], (ROWS, COLS, C), 1.0, 6.0, ((0, 16),))
    return {"image": image, "tissue": tissue, "kernel": kernel, "ln_gain": ln_gain, "w_in": w_in, "w_out": w_out, "layer_scale": layer_scale, "cotangent": cotangent}


EPSILON = 1e-06
ROOT_TWO_PI = 0.7978845608028654
CUBIC_TERM = 0.044715

def gelu_value(inputs):
    tangent = jnp.tanh(ROOT_TWO_PI * (inputs + CUBIC_TERM * inputs * inputs * inputs))
    return 0.5 * inputs * (1.0 + tangent)

def gelu_slope(inputs):
    tangent = jnp.tanh(ROOT_TWO_PI * (inputs + CUBIC_TERM * inputs * inputs * inputs))
    return 0.5 * (1.0 + tangent) + 0.5 * inputs * (1.0 - tangent * tangent) * ROOT_TWO_PI * (1.0 + 3.0 * CUBIC_TERM * inputs * inputs)

def depthwise(padded, kernel, image_rows, image_cols):
    total = jnp.zeros((image_rows, image_cols, kernel.shape[-1]), jnp.float32)
    for row_tap in range(KERNEL):
        for col_tap in range(KERNEL):
            total = total + padded[row_tap:row_tap + image_rows, col_tap:col_tap + image_cols] * kernel[row_tap, col_tap]
    return total

def kernel_terms(padded, grads, image_rows, image_cols):
    collected = []
    for row_tap in range(KERNEL):
        for col_tap in range(KERNEL):
            collected.append(lax.optimization_barrier(jnp.sum(padded[row_tap:row_tap + image_rows, col_tap:col_tap + image_cols] * grads, axis=(0, 1))))
    return jnp.stack(collected)

def reference(image, tissue, kernel, ln_gain, w_in, w_out, layer_scale, cotangent):
    image_rows, image_cols, channels = image.shape
    hidden = w_in.shape[1]
    half_width = KERNEL // 2
    padded = jnp.pad(image.astype(jnp.float32), ((half_width, half_width), (half_width, half_width), (0, 0)))
    filtered = depthwise(padded, kernel, image_rows, image_cols)
    centre = lax.optimization_barrier(jnp.mean(filtered, axis=-1, keepdims=True))
    centered = filtered - centre
    inv_std = lax.rsqrt(lax.optimization_barrier(jnp.mean(centered * centered, axis=-1, keepdims=True)) + EPSILON)
    standard = centered * inv_std
    normed = (standard * ln_gain).astype(jnp.bfloat16)
    tissue_at = jnp.repeat(jnp.repeat(tissue, TILE_ROWS, axis=0), TILE_COLS, axis=1).astype(jnp.float32)[:, :, None]
    upstream = cotangent.astype(jnp.float32)
    grad_out = (tissue_at * layer_scale * upstream).astype(jnp.bfloat16)
    blocks = image_rows // TILE_ROWS
    normed_blocks = normed.reshape(blocks, TILE_ROWS * image_cols, channels)
    grad_blocks = grad_out.reshape(blocks, TILE_ROWS * image_cols, channels)

    def block_step(totals, record):
        grad_in_sum, grad_out_sum = totals
        normed_blk, grad_blk = record
        pre_act = jnp.dot(normed_blk, w_in, preferred_element_type=jnp.float32)
        activation = gelu_value(pre_act).astype(jnp.bfloat16)
        branch = jnp.dot(activation, w_out, preferred_element_type=jnp.float32)
        grad_act = jnp.dot(grad_blk, w_out.T, preferred_element_type=jnp.float32)
        grad_pre = (grad_act * gelu_slope(pre_act)).astype(jnp.bfloat16)
        grad_norm = jnp.dot(grad_pre, w_in.T, preferred_element_type=jnp.float32)
        grad_in_sum = grad_in_sum + jnp.dot(normed_blk.T, grad_pre, preferred_element_type=jnp.float32)
        grad_out_sum = grad_out_sum + jnp.dot(activation.T, grad_blk, preferred_element_type=jnp.float32)
        return ((grad_in_sum, grad_out_sum), (branch, grad_norm))
    start_totals = (jnp.zeros((channels, hidden), jnp.float32), jnp.zeros((hidden, channels), jnp.float32))
    (grad_w_in, grad_w_out), (branch_blocks, norm_blocks) = lax.scan(block_step, start_totals, (normed_blocks, grad_blocks))
    branch = branch_blocks.reshape(image_rows, image_cols, channels)
    grad_norm = norm_blocks.reshape(image_rows, image_cols, channels)
    block_out = (image.astype(jnp.float32) + tissue_at * layer_scale * branch).astype(jnp.bfloat16)
    scale_grad = lax.optimization_barrier(jnp.sum(tissue_at * branch * upstream, axis=(0, 1)))
    gain_grad = lax.optimization_barrier(jnp.sum(grad_norm * standard, axis=(0, 1)))
    grad_std = grad_norm * ln_gain
    grad_conv = (inv_std * (grad_std - lax.optimization_barrier(jnp.mean(grad_std, axis=-1, keepdims=True)) - standard * lax.optimization_barrier(jnp.mean(grad_std * standard, axis=-1, keepdims=True)))).astype(jnp.bfloat16)
    grad_float = grad_conv.astype(jnp.float32)
    kernel_grad = kernel_terms(padded, grad_float, image_rows, image_cols)
    small_grads = jnp.concatenate([kernel_grad, gain_grad[None], scale_grad[None]], axis=0)
    grad_padded = jnp.pad(grad_float, ((half_width, half_width), (half_width, half_width), (0, 0)))
    conv_back = depthwise(grad_padded, kernel[::-1, ::-1], image_rows, image_cols)
    grad_image = (upstream + conv_back).astype(jnp.bfloat16)
    return (block_out, grad_image, grad_w_in, grad_w_out, small_grads)
```

```python
import functools

import jax
import jax.numpy as jnp
from jax import lax
from jax.experimental import pallas as pl
from jax.experimental.pallas import tpu as pltpu
from jax.sharding import PartitionSpec as P

KERNEL = 7
HALF = KERNEL // 2
TILE_COLS = 128
PAD = 16
WIN = 144
FCHUNK = 256

EPSILON = 1e-06
ROOT_TWO_PI = 0.7978845608028654
CUBIC_TERM = 0.044715

BF = jnp.bfloat16
F32 = jnp.float32


def ones_where(shape, rule):
    rows = lax.broadcasted_iota(jnp.int32, shape, 0)
    cols = lax.broadcasted_iota(jnp.int32, shape, 1)
    return jnp.where(rule(rows, cols), 1.0, 0.0).astype(BF)


def mm(a, b, dims=((1,), (0,))):
    return lax.dot_general(a, b, (dims, ((), ())), preferred_element_type=F32)


def other(me, bit):
    step = 1 << bit
    return me + step - 2 * step * ((me // step) % 2)


class Scatter:
    def __init__(self, me, order, bufs, rbufs, ssem, rsem):
        self.me, self.order = me, order
        self.bufs, self.rbufs, self.ssem, self.rsem = bufs, rbufs, ssem, rsem

    def place(self, chunk):
        n = len(self.order)
        return sum(((chunk >> bit) & 1) << (n - 1 - k) for k, bit in enumerate(self.order))

    def halves(self, k):
        half = self.rbufs[k].shape[0]
        mine = (self.me // (1 << self.order[k])) % 2
        return half, mine

    def copy(self, k):
        half, mine = self.halves(k)
        return pltpu.make_async_remote_copy(
            src_ref=self.bufs[k].at[pl.ds((1 - mine) * half, half)],
            dst_ref=self.rbufs[k],
            send_sem=self.ssem.at[k],
            recv_sem=self.rsem.at[k],
            device_id={"row": other(self.me, self.order[k])},
            device_id_type=pl.DeviceIdType.MESH,
        )

    def start(self, k):
        self.copy(k).start()

    def finish(self, k, out_ref):
        self.copy(k).wait()
        half, mine = self.halves(k)
        if k + 1 < len(self.order):
            def step(c, _):
                self.bufs[k + 1][c] = self.bufs[k][mine * half + c] + self.rbufs[k][c]
                return 0

            lax.fori_loop(0, half, step, 0)
            self.start(k + 1)
        else:
            out_ref[...] = self.bufs[k][mine].astype(F32) + self.rbufs[k][0].astype(F32)


def body(
    n, bits,
    tissue_ref, image_ref, kernel_ref, gain_ref, w_in_ref, w_out_ref, scale_ref, cot_ref,
    out_ref, gimg_ref, gwin_ref, gwout_ref, small_ref,
    *scratch,
):
    (ipad, win, kf, kb, shift_f, place_m, place_c, prods, normed_ref, std_ref, istd_ref, grad_ref,
     gbuf, gup, gdn, gshift, kacc, sums, sums_in, pown, pup, pdn) = scratch[:22]
    in_bufs = scratch[22 : 22 + bits]
    in_rbufs = scratch[22 + bits : 22 + 2 * bits]
    out_bufs = scratch[22 + 2 * bits : 22 + 3 * bits]
    out_rbufs = scratch[22 + 3 * bits : 22 + 4 * bits]
    (hs, hr, gs, gr, in_s, in_r, out_s, out_r, sm_s, sm_r) = scratch[22 + 4 * bits :]

    rows, cols, channels = image_ref.shape
    hidden = w_in_ref.shape[1]
    positions = rows * TILE_COLS
    me = lax.axis_index("row")
    has_up = me > 0
    has_dn = me < n - 1

    def signal(target):
        pl.semaphore_signal(
            pltpu.get_barrier_semaphore(), inc=1, device_id={"row": target},
            device_id_type=pl.DeviceIdType.MESH,
        )

    for bit in range(bits):
        signal(other(me, bit))

    @pl.when(has_up)
    def _():
        signal(me - 1)

    @pl.when(has_dn)
    def _():
        signal(me + 1)

    ipad[:, 0:PAD, :] = jnp.zeros((rows + 2 * HALF, PAD, channels), BF)
    ipad[:, PAD + cols :, :] = jnp.zeros((rows + 2 * HALF, PAD, channels), BF)
    edge_rows = jnp.zeros((HALF, cols, channels), BF)
    edge_grad = jnp.zeros(gup.shape, BF)

    @pl.when(me == 0)
    def _():
        ipad[0:HALF, PAD : PAD + cols, :] = edge_rows
        gup[...] = edge_grad

    @pl.when(me == n - 1)
    def _():
        ipad[HALF + rows :, PAD : PAD + cols, :] = edge_rows
        gdn[...] = edge_grad

    count = bits + jnp.where(me > 0, 1, 0) + jnp.where(me < n - 1, 1, 0)
    pl.semaphore_wait(pltpu.get_barrier_semaphore(), count)

    def remote(src, dst, ssem, rsem, target):
        return pltpu.make_async_remote_copy(
            src_ref=src, dst_ref=dst, send_sem=ssem, recv_sem=rsem,
            device_id={"row": target}, device_id_type=pl.DeviceIdType.MESH,
        )

    def halo_dn():
        return remote(image_ref.at[rows - HALF : rows], ipad.at[0:HALF, PAD : PAD + cols],
                      hs.at[0], hr.at[0], me + 1)

    def halo_up():
        return remote(image_ref.at[0:HALF], ipad.at[HALF + rows : rows + 2 * HALF, PAD : PAD + cols],
                      hs.at[1], hr.at[1], me - 1)

    @pl.when(has_dn)
    def _():
        halo_dn().start()

    @pl.when(has_up)
    def _():
        halo_up().start()

    tile = tissue_ref[0, 1]
    flag = tile.astype(F32)
    in_right = jnp.full((1, 1), flag, F32).astype(BF)
    in_left = jnp.full((1, 1), 1.0 - flag, F32).astype(BF)

    def at_tile(ref, r, width):
        left, right = ref[r, 0:width, :], ref[r, TILE_COLS : TILE_COLS + width, :]
        return left * in_left + right * in_right

    ipad[HALF : HALF + rows, PAD : PAD + cols, :] = image_ref[...]
    for i in range(KERNEL):
        for j in range(KERNEL):
            tap = kernel_ref[i, j : j + 1, :]
            kf[i * KERNEL + j] = jnp.broadcast_to(tap, (8, channels))
            kb[i * KERNEL + j] = jnp.broadcast_to(tap, (16, channels)).astype(BF)
    for j in range(KERNEL):
        shift_f[:, j * WIN : (j + 1) * WIN] = ones_where((TILE_COLS, WIN), lambda w, x: x == w + j)
        lanes = slice(j * TILE_COLS, (j + 1) * TILE_COLS)
        low = ones_where((TILE_COLS, TILE_COLS), lambda b, w: w == b - j + HALF)
        right = ones_where((TILE_COLS, TILE_COLS), lambda b, w: w == b - TILE_COLS - j + HALF)
        left = ones_where((TILE_COLS, TILE_COLS), lambda b, w: w == b + TILE_COLS - j + HALF)
        place_m[0:TILE_COLS, lanes] = low
        place_m[TILE_COLS:, lanes] = left
        place_c[0:TILE_COLS, lanes] = right - low
        place_c[TILE_COLS:, lanes] = low - left
    select = ones_where((WIN, WIN + PAD), lambda x, y: y == x + PAD - HALF)
    scale = scale_ref[...]
    gain = gain_ref[...]
    for a in range(rows):
        span = slice(a * TILE_COLS, (a + 1) * TILE_COLS)
        upstream = at_tile(cot_ref, a, TILE_COLS).astype(F32)
        grad_ref[span, :] = (scale * upstream).astype(BF)

    def window(r):
        win[r] = mm(select, at_tile(ipad, r, WIN + PAD)).astype(BF)

    for r in range(HALF, HALF + rows):
        window(r)

    @pl.when(has_up)
    def _():
        halo_dn().wait_recv()

    for r in range(HALF):
        window(r)

    @pl.when(has_dn)
    def _():
        halo_up().wait_recv()

    for r in range(HALF + rows, rows + 2 * HALF):
        window(r)

    def conv_step(c, _):
        at = pl.ds(pl.multiple_of(c * 16, 16), 16)
        for lanes in (slice(0, 128), slice(128, 256)):
            lines = [win[r, at, lanes].astype(F32) for r in range(rows + 2 * HALF)]
            for j in range(KERNEL):
                taps = [kf[i * KERNEL + j, :, lanes] for i in range(KERNEL)]
                for a in range(rows):
                    total = lines[a] * jnp.concatenate([taps[0]] * 2, axis=0)
                    for i in range(1, KERNEL):
                        total = total + lines[a + i] * jnp.concatenate([taps[i]] * 2, axis=0)
                    prods[a, j, at, lanes] = total.astype(BF)
        return 0

    lax.fori_loop(0, WIN // 16, conv_step, 0)

    for a in range(rows):
        span = slice(a * TILE_COLS, (a + 1) * TILE_COLS)
        filtered = mm(shift_f[...], prods[a].reshape(KERNEL * WIN, channels))
        centred = filtered - jnp.mean(filtered, axis=-1, keepdims=True)
        inv_std = lax.rsqrt(jnp.mean(centred * centred, axis=-1, keepdims=True) + EPSILON)
        standard = centred * inv_std
        std_ref[span, :] = standard
        istd_ref[span, :] = inv_std
        normed_ref[span, :] = (standard * gain).astype(BF)

    scat_in = Scatter(me, [0] + list(range(2, bits)) + [1], in_bufs, in_rbufs, in_s, in_r)
    scat_out = Scatter(me, list(range(bits)), out_bufs, out_rbufs, out_s, out_r)
    in_rows = gwin_ref.shape[0]
    out_rows = gwout_ref.shape[0]

    normed = normed_ref[...]
    grads = grad_ref[...]
    branch = jnp.zeros((positions, channels), F32)
    grad_norm = jnp.zeros((positions, channels), F32)
    for f in range(hidden // FCHUNK):
        fs = slice(f * FCHUNK, (f + 1) * FCHUNK)
        w_in = w_in_ref[:, fs]
        w_out = w_out_ref[fs, :]
        z = mm(normed, w_in)
        zz = z * z
        tangent = jnp.tanh(z * (ROOT_TWO_PI + (ROOT_TWO_PI * CUBIC_TERM) * zz))
        half_up = 0.5 + 0.5 * tangent
        act = (z * half_up).astype(BF)
        slope = half_up + z * (half_up * (1.0 - tangent)) * (
            ROOT_TWO_PI + (3.0 * ROOT_TWO_PI * CUBIC_TERM) * zz
        )
        branch = branch + mm(act, w_out)
        grad_pre = (mm(grads, w_out, ((1,), (1,))) * slope).astype(BF)
        grad_norm = grad_norm + mm(grad_pre, w_in, ((1,), (1,)))
        part = mm(act, grads, ((0,), (0,))).astype(BF)
        per = FCHUNK // out_rows
        for q in range(per):
            out_bufs[0][scat_out.place(f * per + q)] = part[q * out_rows : (q + 1) * out_rows]
        part = mm(normed, grad_pre, ((0,), (0,))).astype(BF)
        for q in range(n):
            in_bufs[0][scat_in.place(q), :, fs] = part[q * in_rows : (q + 1) * in_rows]
    scat_out.start(0)
    scat_in.start(0)

    standard = std_ref[...]
    grad_std = grad_norm * gain
    mean_g = jnp.mean(grad_std, axis=-1, keepdims=True)
    mean_s = jnp.mean(grad_std * standard, axis=-1, keepdims=True)
    grad_conv = (istd_ref[...] * (grad_std - mean_g - standard * mean_s)).astype(BF)
    gbuf[16 : 16 + positions, :] = grad_conv
    flags = jnp.full((16, channels), flag, F32).astype(BF)
    gbuf[0:16, :] = flags
    gbuf[16 + positions :, :] = flags
    reach = HALF * TILE_COLS

    def grad_up():
        return remote(gbuf.at[0 : 16 + reach], gdn, gs.at[0], gr.at[0], me - 1)

    def grad_dn():
        return remote(gbuf.at[16 + positions - reach : 32 + positions], gup, gs.at[1], gr.at[1], me + 1)

    @pl.when(has_up)
    def _():
        grad_up().start()

    @pl.when(has_dn)
    def _():
        grad_dn().start()

    scale_sum = jnp.zeros((1, channels), F32)
    for a in range(rows):
        span = slice(a * TILE_COLS, (a + 1) * TILE_COLS)
        upstream = at_tile(cot_ref, a, TILE_COLS).astype(F32)
        scale_sum = scale_sum + jnp.sum(branch[span] * upstream, axis=0, keepdims=True)
        added = scale * branch[span]
        for s in range(2):
            weight = flag if s == 1 else 1.0 - flag
            cs = slice(s * TILE_COLS, (s + 1) * TILE_COLS)
            out_ref[a, cs, :] = (image_ref[a, cs, :].astype(F32) + weight * added).astype(BF)
    gain_sum = jnp.sum(grad_norm * standard, axis=0, keepdims=True)

    scat_out.finish(0, None)
    scat_in.finish(0, None)

    for h in range(rows):
        line = grad_conv[h * TILE_COLS : (h + 1) * TILE_COLS]
        for j in range(KERNEL):
            gshift[j, h] = mm(
                shift_f[:, j * WIN : (j + 1) * WIN], line, ((0,), (0,))
            ).astype(BF)
    kacc[...] = jnp.zeros(kacc.shape, F32)

    def kernel_step(c, _):
        at = pl.ds(pl.multiple_of(c * 16, 16), 16)
        lines = [win[r, at, :] for r in range(rows + 2 * HALF)]
        for j in range(KERNEL):
            shifted = [gshift[j, h, at, :] for h in range(rows)]
            for i in range(KERNEL):
                total = lines[i] * shifted[0]
                for h in range(1, rows):
                    total = total + lines[i + h] * shifted[h]
                total = total.astype(F32)
                kacc[i * KERNEL + j] += total[0:8] + total[8:16]
        return 0

    lax.fori_loop(0, WIN // 16, kernel_step, 0)
    for t in range(KERNEL * KERNEL):
        sums[0, t : t + 1, :] = jnp.sum(kacc[t], axis=0, keepdims=True)
    sums[0, 49:50, :] = gain_sum
    sums[0, 50:51, :] = scale_sum
    sums[0, 51:, :] = jnp.zeros((sums.shape[1] - 51, channels), F32)

    def small(k):
        return remote(sums.at[k], sums_in.at[k], sm_s.at[k], sm_r.at[k], other(me, k))

    small(0).start()
    scat_out.finish(1, None)
    scat_in.finish(1, None)

    def back_step(c, _):
        at = pl.ds(pl.multiple_of(c * 16, 16), 16)
        own = [gbuf[pl.ds(pl.multiple_of(16 + h * TILE_COLS + c * 16, 16), 16), :] for h in range(rows)]
        for j in range(KERNEL):
            taps = [kb[i * KERNEL + j] for i in range(KERNEL)]
            for a in range(rows):
                total = own[0] * taps[a + HALF]
                for r in range(1, rows):
                    total = total + own[r] * taps[a - r + HALF]
                pown[a, j, at, :] = total
        return 0

    lax.fori_loop(0, TILE_COLS // 16, back_step, 0)

    def small_next(k):
        small(k).wait()
        if k + 1 < bits:
            sums[k + 1] = sums[k] + sums_in[k]
            small(k + 1).start()
        else:
            small_ref[...] = (sums[k] + sums_in[k])[: small_ref.shape[0]]

    small_next(0)

    @pl.when(has_up)
    def _():
        grad_dn().wait_recv()

    @pl.when(has_dn)
    def _():
        grad_up().wait_recv()

    def halo_step(c, _):
        at = pl.ds(pl.multiple_of(c * 16, 16), 16)
        above = [gup[pl.ds(pl.multiple_of(u * TILE_COLS + c * 16, 16), 16), :] for u in range(HALF)]
        below = [gdn[pl.ds(pl.multiple_of(16 + u * TILE_COLS + c * 16, 16), 16), :] for u in range(HALF)]
        for j in range(KERNEL):
            taps = [kb[i * KERNEL + j] for i in range(KERNEL)]
            for a in range(HALF):
                total = above[a] * taps[KERNEL - 1]
                for u in range(a + 1, HALF):
                    total = total + above[u] * taps[a - u + KERNEL - 1]
                pup[a, j, at, :] = total
            for a in range(rows - HALF, rows):
                total = below[0] * taps[a + HALF - rows]
                for v in range(1, a + HALF - rows + 1):
                    total = total + below[v] * taps[a + HALF - rows - v]
                pdn[a - (rows - HALF), j, at, :] = total
        return 0

    lax.fori_loop(0, TILE_COLS // 16, halo_step, 0)

    def placing(value):
        return place_m[...] + place_c[...] * value

    depth = KERNEL * TILE_COLS
    at_own = placing(in_right)
    at_up = placing(gup[reach : reach + 1, 0:1])
    at_dn = placing(gdn[0:1, 0:1])
    for a in range(rows):
        total = mm(at_own, pown[a].reshape(depth, channels))
        if a < HALF:
            total = total + mm(at_up, pup[a].reshape(depth, channels))
        if a >= rows - HALF:
            total = total + mm(at_dn, pdn[a - (rows - HALF)].reshape(depth, channels))
        gimg_ref[a] = (cot_ref[a].astype(F32) + total).astype(BF)

    for k in range(2, bits):
        scat_out.finish(k, gwout_ref)
        scat_in.finish(k, gwin_ref)
        small_next(k - 1)
    small_next(bits - 1)

    @pl.when(has_dn)
    def _():
        halo_dn().wait_send()
        grad_dn().wait_send()

    @pl.when(has_up)
    def _():
        halo_up().wait_send()
        grad_up().wait_send()


def shards(n, image, tissue, kernel, ln_gain, w_in, w_out, layer_scale, cotangent):
    rows, cols, channels = image.shape
    hidden = w_in.shape[1]
    bits = n.bit_length() - 1
    in_rows, out_rows = channels // n, hidden // n
    positions = rows * TILE_COLS
    halo = HALF * TILE_COLS + 16
    vmem = pltpu.VMEM
    scratch = [
        vmem((rows + 2 * HALF, cols + 2 * PAD, channels), BF),
        vmem((rows + 2 * HALF, WIN, channels), BF),
        vmem((KERNEL * KERNEL, 8, channels), F32),
        vmem((KERNEL * KERNEL, 16, channels), BF),
        vmem((TILE_COLS, KERNEL * WIN), BF),
        vmem((2 * TILE_COLS, KERNEL * TILE_COLS), BF),
        vmem((2 * TILE_COLS, KERNEL * TILE_COLS), BF),
        vmem((rows, KERNEL, WIN, channels), BF),
        vmem((positions, channels), BF),
        vmem((positions, channels), F32),
        vmem((positions, 1), F32),
        vmem((positions, channels), BF),
        vmem((positions + 32, channels), BF),
        vmem((halo, channels), BF),
        vmem((halo, channels), BF),
        vmem((KERNEL, rows, WIN, channels), BF),
        vmem((KERNEL * KERNEL, 8, channels), F32),
        vmem((bits, 56, channels), F32),
        vmem((bits, 56, channels), F32),
        vmem((rows, KERNEL, TILE_COLS, channels), BF),
        vmem((HALF, KERNEL, TILE_COLS, channels), BF),
        vmem((HALF, KERNEL, TILE_COLS, channels), BF),
    ]
    for shape in ((in_rows, hidden), (out_rows, channels)):
        scratch += [vmem((n >> k,) + shape, BF) for k in range(bits)]
        scratch += [vmem((n >> (k + 1),) + shape, BF) for k in range(bits)]
    dma = pltpu.SemaphoreType.DMA
    scratch += [dma((2,))] * 4 + [dma((bits,))] * 6
    whole = pl.BlockSpec(memory_space=pltpu.VMEM)
    return pl.pallas_call(
        functools.partial(body, n, bits),
        out_shape=(
            jax.ShapeDtypeStruct((rows, cols, channels), BF),
            jax.ShapeDtypeStruct((rows, cols, channels), BF),
            jax.ShapeDtypeStruct((in_rows, hidden), F32),
            jax.ShapeDtypeStruct((out_rows, channels), F32),
            jax.ShapeDtypeStruct((KERNEL * KERNEL + 2, channels), F32),
        ),
        in_specs=[pl.BlockSpec(memory_space=pltpu.SMEM)] + [whole] * 7,
        out_specs=(whole,) * 5,
        scratch_shapes=scratch,
        compiler_params=pltpu.CompilerParams(
            collective_id=0, has_side_effects=True, vmem_limit_bytes=48 * 1024 * 1024
        ),
    )(
        tissue, image, kernel, ln_gain.reshape(1, channels), w_in, w_out,
        layer_scale.reshape(1, channels), cotangent,
    )


def solution(mesh):
    placed = (
        P(("group", "row"), None, None),
        P(("group", "row"), None),
        P(),
        P(),
        P(),
        P(),
        P(),
        P(("group", "row"), None, None),
    )
    return jax.shard_map(
        functools.partial(shards, mesh.shape["row"]),
        mesh=mesh,
        in_specs=placed,
        out_specs=(
            P(("group", "row"), None, None),
            P(("group", "row"), None, None),
            P(("group", "row"), None),
            P(("group", "row"), None),
            P("group", None),
        ),
        check_vma=False,
    )
```

```python
import functools

import jax
import jax.numpy as jnp
from jax import lax
from jax.experimental import pallas as pl
from jax.experimental.pallas import tpu as pltpu
from jax.sharding import PartitionSpec as P

KERNEL = 7
HALF = KERNEL // 2
TILE_COLS = 128
PAD = 16
WIN = 144
FCHUNK = 256

EPSILON = 1e-06
ROOT_TWO_PI = 0.7978845608028654
CUBIC_TERM = 0.044715

BF = jnp.bfloat16
F32 = jnp.float32


def ones_where(shape, rule):
    rows = lax.broadcasted_iota(jnp.int32, shape, 0)
    cols = lax.broadcasted_iota(jnp.int32, shape, 1)
    return jnp.where(rule(rows, cols), 1.0, 0.0).astype(BF)


def mm(a, b, dims=((1,), (0,))):
    return lax.dot_general(a, b, (dims, ((), ())), preferred_element_type=F32)


def other(me, bit):
    step = 1 << bit
    return me + step - 2 * step * ((me // step) % 2)


class Scatter:
    def __init__(self, me, order, bufs, rbufs, ssem, rsem):
        self.me, self.order = me, order
        self.bufs, self.rbufs, self.ssem, self.rsem = bufs, rbufs, ssem, rsem

    def place(self, chunk):
        n = len(self.order)
        return sum(((chunk >> bit) & 1) << (n - 1 - k) for k, bit in enumerate(self.order))

    def halves(self, k):
        half = self.rbufs[k].shape[0]
        mine = (self.me // (1 << self.order[k])) % 2
        return half, mine

    def copy(self, k):
        half, mine = self.halves(k)
        return pltpu.make_async_remote_copy(
            src_ref=self.bufs[k].at[pl.ds((1 - mine) * half, half)],
            dst_ref=self.rbufs[k],
            send_sem=self.ssem.at[k],
            recv_sem=self.rsem.at[k],
            device_id={"row": other(self.me, self.order[k])},
            device_id_type=pl.DeviceIdType.MESH,
        )

    def start(self, k):
        self.copy(k).start()

    def finish(self, k, out_ref):
        self.copy(k).wait()
        half, mine = self.halves(k)
        if k + 1 < len(self.order):
            def step(c, _):
                self.bufs[k + 1][c] = self.bufs[k][mine * half + c] + self.rbufs[k][c]
                return 0

            lax.fori_loop(0, half, step, 0)
            self.start(k + 1)
        else:
            out_ref[...] = self.bufs[k][mine].astype(F32) + self.rbufs[k][0].astype(F32)


def body(
    n, bits,
    tissue_ref, image_ref, kernel_hbm, gain_hbm, w_in_hbm, w_out_hbm, scale_hbm, cot_hbm,
    out_hbm, gimg_hbm, gwin_hbm, gwout_hbm, small_hbm,
    *scratch,
):
    (ipad, win, kf, kb, shift_f, place_m, place_c, prods, normed_ref, std_ref, istd_ref, grad_ref,
     gbuf, gup, gdn, gshift, kacc, sums, sums_in, pown, pup, pdn) = scratch[:22]
    in_bufs = scratch[22 : 22 + bits]
    in_rbufs = scratch[22 + bits : 22 + 2 * bits]
    out_bufs = scratch[22 + 2 * bits : 22 + 3 * bits]
    out_rbufs = scratch[22 + 3 * bits : 22 + 4 * bits]
    (hs, hr, gs, gr, in_s, in_r, out_s, out_r, sm_s, sm_r) = scratch[22 + 4 * bits : 22 + 4 * bits + 10]

    kernel_ref, gain_ref, w_in_ref, w_out_ref, scale_ref, cot_ref, load_sem = scratch[22 + 4 * bits + 10 : -6]
    out_ref, gimg_ref, gwin_ref, gwout_ref, small_ref, store_sem = scratch[-6:]
    stores = [
        pltpu.make_async_copy(src, dst, store_sem.at[k])
        for k, (src, dst) in enumerate((
            (out_ref, out_hbm), (gimg_ref, gimg_hbm), (gwin_ref, gwin_hbm),
            (gwout_ref, gwout_hbm), (small_ref, small_hbm),
        ))
    ]
    rows, cols, channels = image_ref.shape
    hidden = w_in_ref.shape[1]
    positions = rows * TILE_COLS
    me = lax.axis_index("row")
    loads = [
        pltpu.make_async_copy(src, dst, load_sem.at[k])
        for k, (src, dst) in enumerate((
            (image_ref, ipad.at[HALF : HALF + rows, PAD : PAD + cols]),
            (kernel_hbm, kernel_ref), (gain_hbm, gain_ref), (scale_hbm, scale_ref),
            (cot_hbm, cot_ref), (w_in_hbm, w_in_ref), (w_out_hbm, w_out_ref),
        ))
    ]
    for load in loads:
        load.start()
    has_up = me > 0
    has_dn = me < n - 1

    def signal(target):
        pl.semaphore_signal(
            pltpu.get_barrier_semaphore(), inc=1, device_id={"row": target},
            device_id_type=pl.DeviceIdType.MESH,
        )

    for bit in range(bits):
        signal(other(me, bit))

    @pl.when(has_up)
    def _():
        signal(me - 1)

    @pl.when(has_dn)
    def _():
        signal(me + 1)

    ipad[:, 0:PAD, :] = jnp.zeros((rows + 2 * HALF, PAD, channels), BF)
    ipad[:, PAD + cols :, :] = jnp.zeros((rows + 2 * HALF, PAD, channels), BF)
    edge_rows = jnp.zeros((HALF, cols, channels), BF)
    edge_grad = jnp.zeros(gup.shape, BF)

    @pl.when(me == 0)
    def _():
        ipad[0:HALF, PAD : PAD + cols, :] = edge_rows
        gup[...] = edge_grad

    @pl.when(me == n - 1)
    def _():
        ipad[HALF + rows :, PAD : PAD + cols, :] = edge_rows
        gdn[...] = edge_grad

    count = bits + jnp.where(me > 0, 1, 0) + jnp.where(me < n - 1, 1, 0)
    pl.semaphore_wait(pltpu.get_barrier_semaphore(), count)

    def remote(src, dst, ssem, rsem, target):
        return pltpu.make_async_remote_copy(
            src_ref=src, dst_ref=dst, send_sem=ssem, recv_sem=rsem,
            device_id={"row": target}, device_id_type=pl.DeviceIdType.MESH,
        )

    def halo_dn():
        return remote(image_ref.at[rows - HALF : rows], ipad.at[0:HALF, PAD : PAD + cols],
                      hs.at[0], hr.at[0], me + 1)

    def halo_up():
        return remote(image_ref.at[0:HALF], ipad.at[HALF + rows : rows + 2 * HALF, PAD : PAD + cols],
                      hs.at[1], hr.at[1], me - 1)

    @pl.when(has_dn)
    def _():
        halo_dn().start()

    @pl.when(has_up)
    def _():
        halo_up().start()

    tile = tissue_ref[0, 1]
    flag = tile.astype(F32)
    in_right = jnp.full((1, 1), flag, F32).astype(BF)
    in_left = jnp.full((1, 1), 1.0 - flag, F32).astype(BF)

    def at_tile(ref, r, width):
        left, right = ref[r, 0:width, :], ref[r, TILE_COLS : TILE_COLS + width, :]
        return left * in_left + right * in_right

    loads[1].wait()
    for i in range(KERNEL):
        for j in range(KERNEL):
            tap = kernel_ref[i, j : j + 1, :]
            kf[i * KERNEL + j] = jnp.broadcast_to(tap, (8, channels))
            kb[i * KERNEL + j] = jnp.broadcast_to(tap, (16, channels)).astype(BF)
    for j in range(KERNEL):
        shift_f[:, j * WIN : (j + 1) * WIN] = ones_where((TILE_COLS, WIN), lambda w, x: x == w + j)
        lanes = slice(j * TILE_COLS, (j + 1) * TILE_COLS)
        low = ones_where((TILE_COLS, TILE_COLS), lambda b, w: w == b - j + HALF)
        right = ones_where((TILE_COLS, TILE_COLS), lambda b, w: w == b - TILE_COLS - j + HALF)
        left = ones_where((TILE_COLS, TILE_COLS), lambda b, w: w == b + TILE_COLS - j + HALF)
        place_m[0:TILE_COLS, lanes] = low
        place_m[TILE_COLS:, lanes] = left
        place_c[0:TILE_COLS, lanes] = right - low
        place_c[TILE_COLS:, lanes] = low - left
    select = ones_where((WIN, WIN + PAD), lambda x, y: y == x + PAD - HALF)
    for load in loads[2:5]:
        load.wait()
    scale = scale_ref[...]
    gain = gain_ref[...]
    for a in range(rows):
        span = slice(a * TILE_COLS, (a + 1) * TILE_COLS)
        upstream = at_tile(cot_ref, a, TILE_COLS).astype(F32)
        grad_ref[span, :] = (scale * upstream).astype(BF)

    def window(r):
        win[r] = mm(select, at_tile(ipad, r, WIN + PAD)).astype(BF)

    loads[0].wait()
    for r in range(HALF, HALF + rows):
        window(r)

    @pl.when(has_up)
    def _():
        halo_dn().wait_recv()

    for r in range(HALF):
        window(r)

    @pl.when(has_dn)
    def _():
        halo_up().wait_recv()

    for r in range(HALF + rows, rows + 2 * HALF):
        window(r)

    def conv_step(c, _):
        at = pl.ds(pl.multiple_of(c * 16, 16), 16)
        for lanes in (slice(0, 128), slice(128, 256)):
            lines = [win[r, at, lanes].astype(F32) for r in range(rows + 2 * HALF)]
            for j in range(KERNEL):
                taps = [kf[i * KERNEL + j, :, lanes] for i in range(KERNEL)]
                for a in range(rows):
                    total = lines[a] * jnp.concatenate([taps[0]] * 2, axis=0)
                    for i in range(1, KERNEL):
                        total = total + lines[a + i] * jnp.concatenate([taps[i]] * 2, axis=0)
                    prods[a, j, at, lanes] = total.astype(BF)
        return 0

    lax.fori_loop(0, WIN // 16, conv_step, 0)

    for a in range(rows):
        span = slice(a * TILE_COLS, (a + 1) * TILE_COLS)
        filtered = mm(shift_f[...], prods[a].reshape(KERNEL * WIN, channels))
        centred = filtered - jnp.mean(filtered, axis=-1, keepdims=True)
        inv_std = lax.rsqrt(jnp.mean(centred * centred, axis=-1, keepdims=True) + EPSILON)
        standard = centred * inv_std
        std_ref[span, :] = standard
        istd_ref[span, :] = inv_std
        normed_ref[span, :] = (standard * gain).astype(BF)

    scat_in = Scatter(me, [0] + list(range(2, bits)) + [1], in_bufs, in_rbufs, in_s, in_r)
    scat_out = Scatter(me, list(range(bits)), out_bufs, out_rbufs, out_s, out_r)
    in_rows = gwin_ref.shape[0]
    out_rows = gwout_ref.shape[0]

    loads[5].wait()
    loads[6].wait()
    normed = normed_ref[...]
    grads = grad_ref[...]
    branch = jnp.zeros((positions, channels), F32)
    grad_norm = jnp.zeros((positions, channels), F32)
    for f in range(hidden // FCHUNK):
        fs = slice(f * FCHUNK, (f + 1) * FCHUNK)
        w_in = w_in_ref[:, fs]
        w_out = w_out_ref[fs, :]
        z = mm(normed, w_in)
        zz = z * z
        tangent = jnp.tanh(z * (ROOT_TWO_PI + (ROOT_TWO_PI * CUBIC_TERM) * zz))
        half_up = 0.5 + 0.5 * tangent
        act = (z * half_up).astype(BF)
        slope = half_up + z * (half_up * (1.0 - tangent)) * (
            ROOT_TWO_PI + (3.0 * ROOT_TWO_PI * CUBIC_TERM) * zz
        )
        branch = branch + mm(act, w_out)
        grad_pre = (mm(grads, w_out, ((1,), (1,))) * slope).astype(BF)
        grad_norm = grad_norm + mm(grad_pre, w_in, ((1,), (1,)))
        part = mm(act, grads, ((0,), (0,))).astype(BF)
        per = FCHUNK // out_rows
        for q in range(per):
            out_bufs[0][scat_out.place(f * per + q)] = part[q * out_rows : (q + 1) * out_rows]
        part = mm(normed, grad_pre, ((0,), (0,))).astype(BF)
        for q in range(n):
            in_bufs[0][scat_in.place(q), :, fs] = part[q * in_rows : (q + 1) * in_rows]
    scat_out.start(0)
    scat_in.start(0)

    standard = std_ref[...]
    grad_std = grad_norm * gain
    mean_g = jnp.mean(grad_std, axis=-1, keepdims=True)
    mean_s = jnp.mean(grad_std * standard, axis=-1, keepdims=True)
    grad_conv = (istd_ref[...] * (grad_std - mean_g - standard * mean_s)).astype(BF)
    gbuf[16 : 16 + positions, :] = grad_conv
    flags = jnp.full((16, channels), flag, F32).astype(BF)
    gbuf[0:16, :] = flags
    gbuf[16 + positions :, :] = flags
    reach = HALF * TILE_COLS

    def grad_up():
        return remote(gbuf.at[0 : 16 + reach], gdn, gs.at[0], gr.at[0], me - 1)

    def grad_dn():
        return remote(gbuf.at[16 + positions - reach : 32 + positions], gup, gs.at[1], gr.at[1], me + 1)

    @pl.when(has_up)
    def _():
        grad_up().start()

    @pl.when(has_dn)
    def _():
        grad_dn().start()

    scale_sum = jnp.zeros((1, channels), F32)
    for a in range(rows):
        span = slice(a * TILE_COLS, (a + 1) * TILE_COLS)
        upstream = at_tile(cot_ref, a, TILE_COLS).astype(F32)
        scale_sum = scale_sum + jnp.sum(branch[span] * upstream, axis=0, keepdims=True)
        added = scale * branch[span]
        for s in range(2):
            weight = flag if s == 1 else 1.0 - flag
            cs = slice(s * TILE_COLS, (s + 1) * TILE_COLS)
            out_ref[a, cs, :] = (ipad[HALF + a, PAD + cs.start : PAD + cs.stop, :].astype(F32) + weight * added).astype(BF)
    stores[0].start()
    gain_sum = jnp.sum(grad_norm * standard, axis=0, keepdims=True)

    scat_out.finish(0, None)
    scat_in.finish(0, None)

    for h in range(rows):
        line = grad_conv[h * TILE_COLS : (h + 1) * TILE_COLS]
        for j in range(KERNEL):
            gshift[j, h] = mm(
                shift_f[:, j * WIN : (j + 1) * WIN], line, ((0,), (0,))
            ).astype(BF)
    kacc[...] = jnp.zeros(kacc.shape, F32)

    def kernel_step(c, _):
        at = pl.ds(pl.multiple_of(c * 16, 16), 16)
        lines = [win[r, at, :] for r in range(rows + 2 * HALF)]
        for j in range(KERNEL):
            shifted = [gshift[j, h, at, :] for h in range(rows)]
            for i in range(KERNEL):
                total = lines[i] * shifted[0]
                for h in range(1, rows):
                    total = total + lines[i + h] * shifted[h]
                total = total.astype(F32)
                kacc[i * KERNEL + j] += total[0:8] + total[8:16]
        return 0

    lax.fori_loop(0, WIN // 16, kernel_step, 0)
    for t in range(KERNEL * KERNEL):
        sums[0, t : t + 1, :] = jnp.sum(kacc[t], axis=0, keepdims=True)
    sums[0, 49:50, :] = gain_sum
    sums[0, 50:51, :] = scale_sum
    sums[0, 51:, :] = jnp.zeros((sums.shape[1] - 51, channels), F32)

    def small(k):
        return remote(sums.at[k], sums_in.at[k], sm_s.at[k], sm_r.at[k], other(me, k))

    small(0).start()
    scat_out.finish(1, None)
    scat_in.finish(1, None)

    def back_step(c, _):
        at = pl.ds(pl.multiple_of(c * 16, 16), 16)
        own = [gbuf[pl.ds(pl.multiple_of(16 + h * TILE_COLS + c * 16, 16), 16), :] for h in range(rows)]
        for j in range(KERNEL):
            taps = [kb[i * KERNEL + j] for i in range(KERNEL)]
            for a in range(rows):
                total = own[0] * taps[a + HALF]
                for r in range(1, rows):
                    total = total + own[r] * taps[a - r + HALF]
                pown[a, j, at, :] = total
        return 0

    lax.fori_loop(0, TILE_COLS // 16, back_step, 0)

    def small_next(k):
        small(k).wait()
        if k + 1 < bits:
            sums[k + 1] = sums[k] + sums_in[k]
            small(k + 1).start()
        else:
            small_ref[...] = (sums[k] + sums_in[k])[: small_ref.shape[0]]

    small_next(0)
    scat_out.finish(2, gwout_ref)
    scat_in.finish(2, gwin_ref)

    @pl.when(has_up)
    def _():
        grad_dn().wait_recv()

    @pl.when(has_dn)
    def _():
        grad_up().wait_recv()

    def halo_step(c, _):
        at = pl.ds(pl.multiple_of(c * 16, 16), 16)
        above = [gup[pl.ds(pl.multiple_of(u * TILE_COLS + c * 16, 16), 16), :] for u in range(HALF)]
        below = [gdn[pl.ds(pl.multiple_of(16 + u * TILE_COLS + c * 16, 16), 16), :] for u in range(HALF)]
        for j in range(KERNEL):
            taps = [kb[i * KERNEL + j] for i in range(KERNEL)]
            for a in range(HALF):
                total = above[a] * taps[KERNEL - 1]
                for u in range(a + 1, HALF):
                    total = total + above[u] * taps[a - u + KERNEL - 1]
                pup[a, j, at, :] = total
            for a in range(rows - HALF, rows):
                total = below[0] * taps[a + HALF - rows]
                for v in range(1, a + HALF - rows + 1):
                    total = total + below[v] * taps[a + HALF - rows - v]
                pdn[a - (rows - HALF), j, at, :] = total
        return 0

    lax.fori_loop(0, TILE_COLS // 16, halo_step, 0)
    small_next(1)

    def placing(value):
        return place_m[...] + place_c[...] * value

    depth = KERNEL * TILE_COLS
    at_own = placing(in_right)
    at_up = placing(gup[reach : reach + 1, 0:1])
    at_dn = placing(gdn[0:1, 0:1])
    for a in range(rows):
        total = mm(at_own, pown[a].reshape(depth, channels))
        if a < HALF:
            total = total + mm(at_up, pup[a].reshape(depth, channels))
        if a >= rows - HALF:
            total = total + mm(at_dn, pdn[a - (rows - HALF)].reshape(depth, channels))
        gimg_ref[a] = (cot_ref[a].astype(F32) + total).astype(BF)
        if a == 1:
            small_next(2)

    stores[1].start()
    for k in range(3, bits):
        scat_out.finish(k, gwout_ref)
        scat_in.finish(k, gwin_ref)
        small_next(k)
    for store in stores[2:]:
        store.start()

    @pl.when(has_dn)
    def _():
        halo_dn().wait_send()
        grad_dn().wait_send()

    @pl.when(has_up)
    def _():
        halo_up().wait_send()
        grad_up().wait_send()

    for store in stores:
        store.wait()


def copy_out(*refs):
    sem = refs[-1]
    copies = [pltpu.make_async_copy(refs[k], refs[5 + k], sem.at[k]) for k in range(5)]
    for copy in copies:
        copy.start()
    for copy in copies:
        copy.wait()


def shards(n, image, tissue, kernel, ln_gain, w_in, w_out, layer_scale, cotangent):
    rows, cols, channels = image.shape
    hidden = w_in.shape[1]
    bits = n.bit_length() - 1
    in_rows, out_rows = channels // n, hidden // n
    positions = rows * TILE_COLS
    halo = HALF * TILE_COLS + 16
    vmem = pltpu.VMEM
    outputs = (
        jax.ShapeDtypeStruct((rows, cols, channels), BF),
        jax.ShapeDtypeStruct((rows, cols, channels), BF),
        jax.ShapeDtypeStruct((in_rows, hidden), F32),
        jax.ShapeDtypeStruct((out_rows, channels), F32),
        jax.ShapeDtypeStruct((KERNEL * KERNEL + 2, channels), F32),
    )
    scratch = [
        vmem((rows + 2 * HALF, cols + 2 * PAD, channels), BF),
        vmem((rows + 2 * HALF, WIN, channels), BF),
        vmem((KERNEL * KERNEL, 8, channels), F32),
        vmem((KERNEL * KERNEL, 16, channels), BF),
        vmem((TILE_COLS, KERNEL * WIN), BF),
        vmem((2 * TILE_COLS, KERNEL * TILE_COLS), BF),
        vmem((2 * TILE_COLS, KERNEL * TILE_COLS), BF),
        vmem((rows, KERNEL, WIN, channels), BF),
        vmem((positions, channels), BF),
        vmem((positions, channels), F32),
        vmem((positions, 1), F32),
        vmem((positions, channels), BF),
        vmem((positions + 32, channels), BF),
        vmem((halo, channels), BF),
        vmem((halo, channels), BF),
        vmem((KERNEL, rows, WIN, channels), BF),
        vmem((KERNEL * KERNEL, 8, channels), F32),
        vmem((bits, 56, channels), F32),
        vmem((bits, 56, channels), F32),
        vmem((rows, KERNEL, TILE_COLS, channels), BF),
        vmem((HALF, KERNEL, TILE_COLS, channels), BF),
        vmem((HALF, KERNEL, TILE_COLS, channels), BF),
    ]
    for shape in ((in_rows, hidden), (out_rows, channels)):
        scratch += [vmem((n >> k,) + shape, BF) for k in range(bits)]
        scratch += [vmem((n >> (k + 1),) + shape, BF) for k in range(bits)]
    dma = pltpu.SemaphoreType.DMA
    scratch += [dma((2,))] * 4 + [dma((bits,))] * 6
    scratch += [vmem(kernel.shape, F32), vmem((1, channels), F32), vmem(w_in.shape, BF),
                vmem(w_out.shape, BF), vmem((1, channels), F32), vmem(cotangent.shape, BF), dma((7,))]
    scratch += [vmem(r.shape, r.dtype) for r in outputs] + [dma((5,))]
    anywhere = pl.BlockSpec(memory_space=pl.ANY)
    results = pl.pallas_call(
        functools.partial(body, n, bits),
        out_shape=outputs,
        in_specs=[pl.BlockSpec(memory_space=pltpu.SMEM)] + [anywhere] * 7,
        out_specs=(anywhere,) * 5,
        scratch_shapes=scratch,
        compiler_params=pltpu.CompilerParams(
            collective_id=0, has_side_effects=True, vmem_limit_bytes=60 * 1024 * 1024
        ),
    )(
        tissue, image, kernel, ln_gain.reshape(1, channels), w_in, w_out,
        layer_scale.reshape(1, channels), cotangent,
    )
    return pl.pallas_call(
        copy_out,
        out_shape=[jax.ShapeDtypeStruct(r.shape, r.dtype) for r in results],
        in_specs=[anywhere] * 5,
        out_specs=[anywhere] * 5,
        scratch_shapes=[dma((5,))],
        compiler_params=pltpu.CompilerParams(vmem_limit_bytes=60 * 1024 * 1024),
    )(*results)


def solution(mesh):
    placed = (
        P(("group", "row"), None, None),
        P(("group", "row"), None),
        P(),
        P(),
        P(),
        P(),
        P(),
        P(("group", "row"), None, None),
    )
    return jax.shard_map(
        functools.partial(shards, mesh.shape["row"]),
        mesh=mesh,
        in_specs=placed,
        out_specs=(
            P(("group", "row"), None, None),
            P(("group", "row"), None, None),
            P(("group", "row"), None),
            P(("group", "row"), None),
            P("group", None),
        ),
        check_vma=False,
    )
```

```python
import functools

import jax
import jax.numpy as jnp
from jax import lax
from jax.experimental import pallas as pl
from jax.experimental.pallas import tpu as pltpu
from jax.sharding import PartitionSpec as P

KERNEL = 7
HALF = KERNEL // 2
TILE_COLS = 128
PAD = 16
WIN = 144
FCHUNK = 256

EPSILON = 1e-06
ROOT_TWO_PI = 0.7978845608028654
CUBIC_TERM = 0.044715

BF = jnp.bfloat16
F32 = jnp.float32


def ones_where(shape, rule):
    rows = lax.broadcasted_iota(jnp.int32, shape, 0)
    cols = lax.broadcasted_iota(jnp.int32, shape, 1)
    return jnp.where(rule(rows, cols), 1.0, 0.0).astype(BF)


def mm(a, b, dims=((1,), (0,))):
    return lax.dot_general(a, b, (dims, ((), ())), preferred_element_type=F32)


def other(me, bit):
    step = 1 << bit
    return me + step - 2 * step * ((me // step) % 2)


class Scatter:
    def __init__(self, me, order, bufs, rbufs, ssem, rsem):
        self.me, self.order = me, order
        self.bufs, self.rbufs, self.ssem, self.rsem = bufs, rbufs, ssem, rsem

    def place(self, chunk):
        return (chunk % 2) * self.rbufs[0].shape[0] + chunk // 2

    def place_next(self, chunk):
        n = len(self.order)
        return sum(((chunk >> bit) & 1) << (n - 1 - k) for k, bit in enumerate(self.order) if k)

    def halves(self, k):
        half = self.rbufs[k].shape[0]
        mine = (self.me // (1 << self.order[k])) % 2
        return half, mine

    def copy(self, k):
        half, mine = self.halves(k)
        return pltpu.make_async_remote_copy(
            src_ref=self.bufs[k].at[pl.ds((1 - mine) * half, half)],
            dst_ref=self.rbufs[k],
            send_sem=self.ssem.at[k],
            recv_sem=self.rsem.at[k],
            device_id={"row": other(self.me, self.order[k])},
            device_id_type=pl.DeviceIdType.MESH,
        )

    def start(self, k):
        self.copy(k).start()

    def part(self, index, sems, picks):
        half, mine = self.halves(0)
        first, *rest = picks
        return pltpu.make_async_remote_copy(
            src_ref=self.bufs[0].at[(pl.ds((1 - mine) * half + first.start, first.size), *rest)],
            dst_ref=self.rbufs[0].at[(first, *rest)],
            send_sem=sems[0].at[index],
            recv_sem=sems[1].at[index],
            device_id={"row": other(self.me, self.order[0])},
            device_id_type=pl.DeviceIdType.MESH,
        )

    def finish_parts(self, parts):
        for part in parts:
            part.wait()
        half, mine = self.halves(0)
        for e in range(half):
            self.bufs[1][self.place_next(2 * e)] = self.bufs[0][mine * half + e] + self.rbufs[0][e]
        self.start(1)

    def finish(self, k, out_ref):
        self.copy(k).wait()
        half, mine = self.halves(k)
        if k + 1 < len(self.order):
            def step(c, _):
                self.bufs[k + 1][c] = self.bufs[k][mine * half + c] + self.rbufs[k][c]
                return 0

            lax.fori_loop(0, half, step, 0)
            self.start(k + 1)
        else:
            out_ref[...] = self.bufs[k][mine].astype(F32) + self.rbufs[k][0].astype(F32)


def body(
    n, bits,
    tissue_ref, image_ref, kernel_hbm, gain_hbm, w_in_hbm, w_out_hbm, scale_hbm, cot_hbm,
    out_hbm, gimg_hbm, gwin_hbm, gwout_hbm, small_hbm,
    *scratch,
):
    (ipad, win, kf, kb, shift_f, place_m, place_c, prods, normed_ref, std_ref, istd_ref, grad_ref,
     gbuf, gup, gdn, gshift, kacc, sums, sums_in, pown, pup, pdn) = scratch[:22]
    in_bufs = scratch[22 : 22 + bits]
    in_rbufs = scratch[22 + bits : 22 + 2 * bits]
    out_bufs = scratch[22 + 2 * bits : 22 + 3 * bits]
    out_rbufs = scratch[22 + 3 * bits : 22 + 4 * bits]
    (hs, hr, gs, gr, in_s, in_r, out_s, out_r, sm_s, sm_r) = scratch[22 + 4 * bits : 22 + 4 * bits + 10]

    kernel_ref, gain_ref, w_in_ref, w_out_ref, scale_ref, cot_ref, load_sem = scratch[22 + 4 * bits + 10 : -12]
    out_ref, gimg_ref, gwin_ref, gwout_ref, small_ref, store_sem = scratch[-6:]
    in0_s, in0_r, out0_s, out0_r, shift_b, conv_part = scratch[-12:-6]
    stores = [
        pltpu.make_async_copy(src, dst, store_sem.at[k])
        for k, (src, dst) in enumerate((
            (out_ref, out_hbm), (gimg_ref, gimg_hbm), (gwin_ref, gwin_hbm),
            (gwout_ref, gwout_hbm), (small_ref, small_hbm),
        ))
    ]
    rows, cols, channels = image_ref.shape
    hidden = w_in_ref.shape[1]
    positions = rows * TILE_COLS
    me = lax.axis_index("row")
    loads = [
        pltpu.make_async_copy(src, dst, load_sem.at[k])
        for k, (src, dst) in enumerate((
            (image_ref, ipad.at[HALF : HALF + rows, PAD : PAD + cols]),
            (kernel_hbm, kernel_ref), (gain_hbm, gain_ref), (scale_hbm, scale_ref),
            (cot_hbm, cot_ref), (w_in_hbm, w_in_ref), (w_out_hbm, w_out_ref),
        ))
    ]
    for load in loads:
        load.start()
    has_up = me > 0
    has_dn = me < n - 1

    def signal(target):
        pl.semaphore_signal(
            pltpu.get_barrier_semaphore(), inc=1, device_id={"row": target},
            device_id_type=pl.DeviceIdType.MESH,
        )

    for bit in range(bits):
        signal(other(me, bit))

    @pl.when(has_up)
    def _():
        signal(me - 1)

    @pl.when(has_dn)
    def _():
        signal(me + 1)

    ipad[:, 0:PAD, :] = jnp.zeros((rows + 2 * HALF, PAD, channels), BF)
    ipad[:, PAD + cols :, :] = jnp.zeros((rows + 2 * HALF, PAD, channels), BF)
    edge_rows = jnp.zeros((HALF, cols, channels), BF)
    edge_grad = jnp.zeros(gup.shape, BF)

    @pl.when(me == 0)
    def _():
        ipad[0:HALF, PAD : PAD + cols, :] = edge_rows
        gup[...] = edge_grad

    @pl.when(me == n - 1)
    def _():
        ipad[HALF + rows :, PAD : PAD + cols, :] = edge_rows
        gdn[...] = edge_grad

    count = bits + jnp.where(me > 0, 1, 0) + jnp.where(me < n - 1, 1, 0)
    pl.semaphore_wait(pltpu.get_barrier_semaphore(), count)

    def remote(src, dst, ssem, rsem, target):
        return pltpu.make_async_remote_copy(
            src_ref=src, dst_ref=dst, send_sem=ssem, recv_sem=rsem,
            device_id={"row": target}, device_id_type=pl.DeviceIdType.MESH,
        )

    def halo_dn():
        return remote(image_ref.at[rows - HALF : rows], ipad.at[0:HALF, PAD : PAD + cols],
                      hs.at[0], hr.at[0], me + 1)

    def halo_up():
        return remote(image_ref.at[0:HALF], ipad.at[HALF + rows : rows + 2 * HALF, PAD : PAD + cols],
                      hs.at[1], hr.at[1], me - 1)

    @pl.when(has_dn)
    def _():
        halo_dn().start()

    @pl.when(has_up)
    def _():
        halo_up().start()

    tile = tissue_ref[0, 1]
    flag = tile.astype(F32)
    in_right = jnp.full((1, 1), flag, F32).astype(BF)
    in_left = jnp.full((1, 1), 1.0 - flag, F32).astype(BF)

    def at_tile(ref, r, width):
        left, right = ref[r, 0:width, :], ref[r, TILE_COLS : TILE_COLS + width, :]
        return left * in_left + right * in_right

    loads[1].wait()
    for i in range(KERNEL):
        for j in range(KERNEL):
            tap = kernel_ref[i, j : j + 1, :]
            kf[i * KERNEL + j] = jnp.broadcast_to(tap, (8, channels))
            kb[i * KERNEL + j] = jnp.broadcast_to(tap, (16, channels)).astype(BF)
    for j in range(KERNEL):
        shift_f[:, j * WIN : (j + 1) * WIN] = ones_where((TILE_COLS, WIN), lambda w, x: x == w + j)
        shift_b[j] = ones_where((WIN, TILE_COLS), lambda x, w: x == w + j)
        lanes = slice(j * TILE_COLS, (j + 1) * TILE_COLS)
        low = ones_where((TILE_COLS, TILE_COLS), lambda b, w: w == b - j + HALF)
        right = ones_where((TILE_COLS, TILE_COLS), lambda b, w: w == b - TILE_COLS - j + HALF)
        left = ones_where((TILE_COLS, TILE_COLS), lambda b, w: w == b + TILE_COLS - j + HALF)
        place_m[0:TILE_COLS, lanes] = low
        place_m[TILE_COLS:, lanes] = left
        place_c[0:TILE_COLS, lanes] = right - low
        place_c[TILE_COLS:, lanes] = low - left
    select = ones_where((WIN, WIN + PAD), lambda x, y: y == x + PAD - HALF)
    for load in loads[2:5]:
        load.wait()
    scale = scale_ref[...]
    gain = gain_ref[...]
    for a in range(rows):
        span = slice(a * TILE_COLS, (a + 1) * TILE_COLS)
        upstream = at_tile(cot_ref, a, TILE_COLS).astype(F32)
        grad_ref[span, :] = (scale * upstream).astype(BF)

    def window(r):
        win[r] = mm(select, at_tile(ipad, r, WIN + PAD)).astype(BF)

    loads[0].wait()
    for r in range(HALF, HALF + rows):
        window(r)

    LANES = (slice(0, 128), slice(128, 256))

    def tap(i, j, lanes):
        one = kf[i * KERNEL + j, :, lanes]
        return jnp.concatenate([one, one], axis=0)

    def conv_own(c, _):
        at = pl.ds(pl.multiple_of(c * 16, 16), 16)
        for lanes in LANES:
            lines = [win[HALF + r, at, lanes].astype(F32) for r in range(rows)]
            for j in range(KERNEL):
                taps = [tap(i, j, lanes) for i in range(KERNEL)]
                for a in range(rows):
                    total = lines[0] * taps[HALF - a]
                    for r in range(1, rows):
                        total = total + lines[r] * taps[HALF + r - a]
                    conv_part[a, j, at, lanes] = total
        return 0

    lax.fori_loop(0, WIN // 16, conv_own, 0)

    @pl.when(has_up)
    def _():
        halo_dn().wait_recv()

    for r in range(HALF):
        window(r)

    @pl.when(has_dn)
    def _():
        halo_up().wait_recv()

    for r in range(HALF + rows, rows + 2 * HALF):
        window(r)

    def conv_halo(c, _):
        at = pl.ds(pl.multiple_of(c * 16, 16), 16)
        for lanes in LANES:
            lines = {
                r: win[r, at, lanes].astype(F32)
                for r in range(rows + 2 * HALF) if not HALF <= r < HALF + rows
            }
            for j in range(KERNEL):
                taps = [tap(i, j, lanes) for i in range(KERNEL)]
                for a in range(rows):
                    total = conv_part[a, j, at, lanes]
                    for r in lines:
                        if 0 <= r - a < KERNEL:
                            total = total + lines[r] * taps[r - a]
                    prods[a, j, at, lanes] = total.astype(BF)
        return 0

    lax.fori_loop(0, WIN // 16, conv_halo, 0)

    for a in range(rows):
        span = slice(a * TILE_COLS, (a + 1) * TILE_COLS)
        filtered = mm(shift_f[...], prods[a].reshape(KERNEL * WIN, channels))
        centred = filtered - jnp.mean(filtered, axis=-1, keepdims=True)
        inv_std = lax.rsqrt(jnp.mean(centred * centred, axis=-1, keepdims=True) + EPSILON)
        standard = centred * inv_std
        std_ref[span, :] = standard
        istd_ref[span, :] = inv_std
        normed_ref[span, :] = (standard * gain).astype(BF)

    scat_in = Scatter(me, [0] + list(range(2, bits)) + [1], in_bufs, in_rbufs, in_s, in_r)
    scat_out = Scatter(me, list(range(bits)), out_bufs, out_rbufs, out_s, out_r)
    in_rows = gwin_ref.shape[0]
    out_rows = gwout_ref.shape[0]

    loads[5].wait()
    loads[6].wait()
    normed = normed_ref[...]
    grads = grad_ref[...]
    branch = jnp.zeros((positions, channels), F32)
    grad_norm = jnp.zeros((positions, channels), F32)
    normed_t = normed.T
    out_parts, in_parts = [], []
    for f in range(hidden // FCHUNK):
        fs = slice(f * FCHUNK, (f + 1) * FCHUNK)
        w_in = w_in_ref[:, fs]
        w_out = w_out_ref[fs, :]
        z = mm(normed, w_in)
        zz = z * z
        tangent = jnp.tanh(z * (ROOT_TWO_PI + (ROOT_TWO_PI * CUBIC_TERM) * zz))
        half_up = 0.5 + 0.5 * tangent
        act = (z * half_up).astype(BF)
        slope = half_up + z * (half_up * (1.0 - tangent)) * (
            ROOT_TWO_PI + (3.0 * ROOT_TWO_PI * CUBIC_TERM) * zz
        )
        branch = branch + mm(act, w_out)
        grad_pre = (mm(grads, w_out, ((1,), (1,))) * slope).astype(BF)
        grad_norm = grad_norm + mm(grad_pre, w_in, ((1,), (1,)))
        part = mm(act, grads, ((0,), (0,))).astype(BF)
        per = FCHUNK // out_rows
        for q in range(per):
            out_bufs[0][scat_out.place(f * per + q)] = part[q * out_rows : (q + 1) * out_rows]
        part = mm(normed_t, grad_pre).astype(BF)
        for q in range(n):
            in_bufs[0][scat_in.place(q), :, fs] = part[q * in_rows : (q + 1) * in_rows]
        out_parts.append(scat_out.part(f, (out0_s, out0_r), (pl.ds(f * per // 2, per // 2),)))
        in_parts.append(scat_in.part(f, (in0_s, in0_r), (pl.ds(0, n // 2), slice(None), fs)))
        out_parts[-1].start()
        in_parts[-1].start()

    standard = std_ref[...]
    grad_std = grad_norm * gain
    mean_g = jnp.mean(grad_std, axis=-1, keepdims=True)
    mean_s = jnp.mean(grad_std * standard, axis=-1, keepdims=True)
    grad_conv = (istd_ref[...] * (grad_std - mean_g - standard * mean_s)).astype(BF)
    gbuf[16 : 16 + positions, :] = grad_conv
    flags = jnp.full((16, channels), flag, F32).astype(BF)
    gbuf[0:16, :] = flags
    gbuf[16 + positions :, :] = flags
    reach = HALF * TILE_COLS

    def grad_up():
        return remote(gbuf.at[0 : 16 + reach], gdn, gs.at[0], gr.at[0], me - 1)

    def grad_dn():
        return remote(gbuf.at[16 + positions - reach : 32 + positions], gup, gs.at[1], gr.at[1], me + 1)

    @pl.when(has_up)
    def _():
        grad_up().start()

    @pl.when(has_dn)
    def _():
        grad_dn().start()

    scat_out.finish_parts(out_parts)
    scat_in.finish_parts(in_parts)

    scale_sum = jnp.zeros((1, channels), F32)
    for a in range(rows):
        span = slice(a * TILE_COLS, (a + 1) * TILE_COLS)
        upstream = at_tile(cot_ref, a, TILE_COLS).astype(F32)
        scale_sum = scale_sum + jnp.sum(branch[span] * upstream, axis=0, keepdims=True)
        added = scale * branch[span]
        for s in range(2):
            weight = flag if s == 1 else 1.0 - flag
            cs = slice(s * TILE_COLS, (s + 1) * TILE_COLS)
            out_ref[a, cs, :] = (ipad[HALF + a, PAD + cs.start : PAD + cs.stop, :].astype(F32) + weight * added).astype(BF)
    stores[0].start()
    gain_sum = jnp.sum(grad_norm * standard, axis=0, keepdims=True)

    for h in range(rows):
        line = grad_conv[h * TILE_COLS : (h + 1) * TILE_COLS]
        for j in range(KERNEL):
            gshift[j, h] = mm(shift_b[j], line).astype(BF)
    kacc[...] = jnp.zeros(kacc.shape, F32)

    def kernel_step(c, _):
        at = pl.ds(pl.multiple_of(c * 16, 16), 16)
        lines = [win[r, at, :] for r in range(rows + 2 * HALF)]
        for j in range(KERNEL):
            shifted = [gshift[j, h, at, :] for h in range(rows)]
            for i in range(KERNEL):
                total = lines[i] * shifted[0]
                for h in range(1, rows):
                    total = total + lines[i + h] * shifted[h]
                total = total.astype(F32)
                kacc[i * KERNEL + j] += total[0:8] + total[8:16]
        return 0

    lax.fori_loop(0, WIN // 16, kernel_step, 0)
    for t in range(KERNEL * KERNEL):
        sums[0, t : t + 1, :] = jnp.sum(kacc[t], axis=0, keepdims=True)
    sums[0, 49:50, :] = gain_sum
    sums[0, 50:51, :] = scale_sum
    sums[0, 51:, :] = jnp.zeros((sums.shape[1] - 51, channels), F32)

    def small(k):
        return remote(sums.at[k], sums_in.at[k], sm_s.at[k], sm_r.at[k], other(me, k))

    small(0).start()
    scat_out.finish(1, None)
    scat_in.finish(1, None)

    def back_step(c, _):
        at = pl.ds(pl.multiple_of(c * 16, 16), 16)
        own = [gbuf[pl.ds(pl.multiple_of(16 + h * TILE_COLS + c * 16, 16), 16), :] for h in range(rows)]
        for j in range(KERNEL):
            taps = [kb[i * KERNEL + j] for i in range(KERNEL)]
            for a in range(rows):
                total = own[0] * taps[a + HALF]
                for r in range(1, rows):
                    total = total + own[r] * taps[a - r + HALF]
                pown[a, j, at, :] = total
        return 0

    lax.fori_loop(0, TILE_COLS // 16, back_step, 0)

    def small_next(k):
        small(k).wait()
        if k + 1 < bits:
            sums[k + 1] = sums[k] + sums_in[k]
            small(k + 1).start()
        else:
            small_ref[...] = (sums[k] + sums_in[k])[: small_ref.shape[0]]

    small_next(0)
    scat_out.finish(2, gwout_ref)
    scat_in.finish(2, gwin_ref)

    @pl.when(has_up)
    def _():
        grad_dn().wait_recv()

    @pl.when(has_dn)
    def _():
        grad_up().wait_recv()

    def halo_step(c, _):
        at = pl.ds(pl.multiple_of(c * 16, 16), 16)
        above = [gup[pl.ds(pl.multiple_of(u * TILE_COLS + c * 16, 16), 16), :] for u in range(HALF)]
        below = [gdn[pl.ds(pl.multiple_of(16 + u * TILE_COLS + c * 16, 16), 16), :] for u in range(HALF)]
        for j in range(KERNEL):
            taps = [kb[i * KERNEL + j] for i in range(KERNEL)]
            for a in range(HALF):
                total = above[a] * taps[KERNEL - 1]
                for u in range(a + 1, HALF):
                    total = total + above[u] * taps[a - u + KERNEL - 1]
                pup[a, j, at, :] = total
            for a in range(rows - HALF, rows):
                total = below[0] * taps[a + HALF - rows]
                for v in range(1, a + HALF - rows + 1):
                    total = total + below[v] * taps[a + HALF - rows - v]
                pdn[a - (rows - HALF), j, at, :] = total
        return 0

    lax.fori_loop(0, TILE_COLS // 16, halo_step, 0)
    small_next(1)

    def placing(value):
        return place_m[...] + place_c[...] * value

    depth = KERNEL * TILE_COLS
    at_own = placing(in_right)
    at_up = placing(gup[reach : reach + 1, 0:1])
    at_dn = placing(gdn[0:1, 0:1])
    for a in range(rows):
        total = mm(at_own, pown[a].reshape(depth, channels))
        if a < HALF:
            total = total + mm(at_up, pup[a].reshape(depth, channels))
        if a >= rows - HALF:
            total = total + mm(at_dn, pdn[a - (rows - HALF)].reshape(depth, channels))
        gimg_ref[a] = (cot_ref[a].astype(F32) + total).astype(BF)
        if a == 1:
            small_next(2)

    stores[1].start()
    for k in range(3, bits):
        scat_out.finish(k, gwout_ref)
        scat_in.finish(k, gwin_ref)
        small_next(k)
    for store in stores[2:]:
        store.start()

    @pl.when(has_dn)
    def _():
        halo_dn().wait_send()
        grad_dn().wait_send()

    @pl.when(has_up)
    def _():
        halo_up().wait_send()
        grad_up().wait_send()

    for store in stores:
        store.wait()


def copy_out(*refs):
    held, in_sem, out_sem = refs[10:15], refs[15], refs[16]
    reads = [pltpu.make_async_copy(refs[k], held[k], in_sem.at[k]) for k in range(5)]
    writes = [pltpu.make_async_copy(held[k], refs[5 + k], out_sem.at[k]) for k in range(5)]
    for read in reads:
        read.start()
    for read, write in zip(reads, writes):
        read.wait()
        write.start()
    for write in writes:
        write.wait()


def shards(n, image, tissue, kernel, ln_gain, w_in, w_out, layer_scale, cotangent):
    rows, cols, channels = image.shape
    hidden = w_in.shape[1]
    bits = n.bit_length() - 1
    in_rows, out_rows = channels // n, hidden // n
    positions = rows * TILE_COLS
    halo = HALF * TILE_COLS + 16
    vmem = pltpu.VMEM
    outputs = (
        jax.ShapeDtypeStruct((rows, cols, channels), BF),
        jax.ShapeDtypeStruct((rows, cols, channels), BF),
        jax.ShapeDtypeStruct((in_rows, hidden), F32),
        jax.ShapeDtypeStruct((out_rows, channels), F32),
        jax.ShapeDtypeStruct((KERNEL * KERNEL + 2, channels), F32),
    )
    scratch = [
        vmem((rows + 2 * HALF, cols + 2 * PAD, channels), BF),
        vmem((rows + 2 * HALF, WIN, channels), BF),
        vmem((KERNEL * KERNEL, 8, channels), F32),
        vmem((KERNEL * KERNEL, 16, channels), BF),
        vmem((TILE_COLS, KERNEL * WIN), BF),
        vmem((2 * TILE_COLS, KERNEL * TILE_COLS), BF),
        vmem((2 * TILE_COLS, KERNEL * TILE_COLS), BF),
        vmem((rows, KERNEL, WIN, channels), BF),
        vmem((positions, channels), BF),
        vmem((positions, channels), F32),
        vmem((positions, 1), F32),
        vmem((positions, channels), BF),
        vmem((positions + 32, channels), BF),
        vmem((halo, channels), BF),
        vmem((halo, channels), BF),
        vmem((KERNEL, rows, WIN, channels), BF),
        vmem((KERNEL * KERNEL, 8, channels), F32),
        vmem((bits, 56, channels), F32),
        vmem((bits, 56, channels), F32),
        vmem((rows, KERNEL, TILE_COLS, channels), BF),
        vmem((HALF, KERNEL, TILE_COLS, channels), BF),
        vmem((HALF, KERNEL, TILE_COLS, channels), BF),
    ]
    for shape in ((in_rows, hidden), (out_rows, channels)):
        scratch += [vmem((n >> k,) + shape, BF) for k in range(bits)]
        scratch += [vmem((n >> (k + 1),) + shape, BF) for k in range(bits)]
    dma = pltpu.SemaphoreType.DMA
    scratch += [dma((2,))] * 4 + [dma((bits,))] * 6
    scratch += [vmem(kernel.shape, F32), vmem((1, channels), F32), vmem(w_in.shape, BF),
                vmem(w_out.shape, BF), vmem((1, channels), F32), vmem(cotangent.shape, BF), dma((7,))]
    scratch += [dma((hidden // FCHUNK,))] * 4
    scratch += [vmem((KERNEL, WIN, TILE_COLS), BF), vmem((rows, KERNEL, WIN, channels), F32)]
    scratch += [vmem(r.shape, r.dtype) for r in outputs] + [dma((5,))]
    anywhere = pl.BlockSpec(memory_space=pl.ANY)
    results = pl.pallas_call(
        functools.partial(body, n, bits),
        out_shape=outputs,
        in_specs=[pl.BlockSpec(memory_space=pltpu.SMEM)] + [anywhere] * 7,
        out_specs=(anywhere,) * 5,
        scratch_shapes=scratch,
        compiler_params=pltpu.CompilerParams(
            collective_id=0, has_side_effects=True, vmem_limit_bytes=60 * 1024 * 1024
        ),
    )(
        tissue, image, kernel, ln_gain.reshape(1, channels), w_in, w_out,
        layer_scale.reshape(1, channels), cotangent,
    )
    return pl.pallas_call(
        copy_out,
        out_shape=[jax.ShapeDtypeStruct(r.shape, r.dtype) for r in results],
        in_specs=[anywhere] * 5,
        out_specs=[anywhere] * 5,
        scratch_shapes=[vmem(r.shape, r.dtype) for r in results] + [dma((5,))] * 2,
        compiler_params=pltpu.CompilerParams(vmem_limit_bytes=60 * 1024 * 1024),
    )(*results)


def solution(mesh):
    placed = (
        P(("group", "row"), None, None),
        P(("group", "row"), None),
        P(),
        P(),
        P(),
        P(),
        P(),
        P(("group", "row"), None, None),
    )
    return jax.shard_map(
        functools.partial(shards, mesh.shape["row"]),
        mesh=mesh,
        in_specs=placed,
        out_specs=(
            P(("group", "row"), None, None),
            P(("group", "row"), None, None),
            P(("group", "row"), None),
            P(("group", "row"), None),
            P("group", None),
        ),
        check_vma=False,
    )
```

```python
import functools

import jax
import jax.numpy as jnp
from jax import lax
from jax.experimental import pallas as pl
from jax.experimental.pallas import tpu as pltpu
from jax.sharding import PartitionSpec as P

KERNEL = 7
HALF = KERNEL // 2
TILE_COLS = 128
PAD = 16
WIN = 144
FCHUNK = 256
BLOCK = 32

EPSILON = 1e-06
ROOT_TWO_PI = 0.7978845608028654
CUBIC_TERM = 0.044715

BF = jnp.bfloat16
F32 = jnp.float32


def ones_where(shape, rule):
    rows = lax.broadcasted_iota(jnp.int32, shape, 0)
    cols = lax.broadcasted_iota(jnp.int32, shape, 1)
    return jnp.where(rule(rows, cols), 1.0, 0.0).astype(BF)


def mm(a, b, dims=((1,), (0,))):
    return lax.dot_general(a, b, (dims, ((), ())), preferred_element_type=F32)


def other(me, bit):
    step = 1 << bit
    return me + step - 2 * step * ((me // step) % 2)


class Scatter:
    def __init__(self, me, order, bufs, rbufs, ssem, rsem):
        self.me, self.order = me, order
        self.bufs, self.rbufs, self.ssem, self.rsem = bufs, rbufs, ssem, rsem

    def place(self, chunk):
        return (chunk % 2) * self.rbufs[0].shape[0] + chunk // 2

    def place_next(self, chunk):
        n = len(self.order)
        return sum(((chunk >> bit) & 1) << (n - 1 - k) for k, bit in enumerate(self.order) if k)

    def halves(self, k):
        half = self.rbufs[k].shape[0]
        mine = (self.me // (1 << self.order[k])) % 2
        return half, mine

    def copy(self, k):
        half, mine = self.halves(k)
        return pltpu.make_async_remote_copy(
            src_ref=self.bufs[k].at[pl.ds((1 - mine) * half, half)],
            dst_ref=self.rbufs[k],
            send_sem=self.ssem.at[k],
            recv_sem=self.rsem.at[k],
            device_id={"row": other(self.me, self.order[k])},
            device_id_type=pl.DeviceIdType.MESH,
        )

    def start(self, k):
        self.copy(k).start()

    def part(self, index, sems, picks):
        half, mine = self.halves(0)
        first, *rest = picks
        return pltpu.make_async_remote_copy(
            src_ref=self.bufs[0].at[(pl.ds((1 - mine) * half + first.start, first.size), *rest)],
            dst_ref=self.rbufs[0].at[(first, *rest)],
            send_sem=sems[0].at[index],
            recv_sem=sems[1].at[index],
            device_id={"row": other(self.me, self.order[0])},
            device_id_type=pl.DeviceIdType.MESH,
        )

    def finish_parts(self, parts):
        for part in parts:
            part.wait()
        half, mine = self.halves(0)
        for e in range(half):
            self.bufs[1][self.place_next(2 * e)] = self.bufs[0][mine * half + e] + self.rbufs[0][e]
        self.start(1)

    def finish(self, k, out_ref):
        self.copy(k).wait()
        half, mine = self.halves(k)
        if k + 1 < len(self.order):
            def step(c, _):
                self.bufs[k + 1][c] = self.bufs[k][mine * half + c] + self.rbufs[k][c]
                return 0

            lax.fori_loop(0, half, step, 0)
            self.start(k + 1)
        else:
            out_ref[...] = self.bufs[k][mine].astype(F32) + self.rbufs[k][0].astype(F32)


def body(
    n, bits,
    tissue_ref, image_ref, kernel_hbm, gain_hbm, w_in_hbm, w_out_hbm, scale_hbm, cot_hbm,
    out_hbm, gimg_hbm, gwin_hbm, gwout_hbm, small_hbm,
    *scratch,
):
    (z_ref, back_ref, act_ref, pre_ref, branch_ref, ipad, win, kf, kb, shift_f, place_m, place_c, prods, normed_ref, std_ref, istd_ref, grad_ref,
     gbuf, gup, gdn, gshift, kacc, sums, sums_in, pown, pup, pdn) = scratch[:27]
    in_bufs = scratch[27 : 27 + bits]
    in_rbufs = scratch[27 + bits : 27 + 2 * bits]
    out_bufs = scratch[27 + 2 * bits : 27 + 3 * bits]
    out_rbufs = scratch[27 + 3 * bits : 27 + 4 * bits]
    (hs, hr, gs, gr, in_s, in_r, out_s, out_r, sm_s, sm_r) = scratch[27 + 4 * bits : 27 + 4 * bits + 10]

    kernel_ref, gain_ref, w_in_ref, w_out_ref, scale_ref, cot_ref, load_sem = scratch[27 + 4 * bits + 10 : -12]
    out_ref, gimg_ref, gwin_ref, gwout_ref, small_ref, store_sem = scratch[-6:]
    in0_s, in0_r, out0_s, out0_r, shift_b, conv_part = scratch[-12:-6]
    stores = [
        pltpu.make_async_copy(src, dst, store_sem.at[k])
        for k, (src, dst) in enumerate((
            (out_ref, out_hbm), (gimg_ref, gimg_hbm), (gwin_ref, gwin_hbm),
            (gwout_ref, gwout_hbm), (small_ref, small_hbm),
        ))
    ]
    rows, cols, channels = image_ref.shape
    hidden = w_in_ref.shape[1]
    positions = rows * TILE_COLS
    me = lax.axis_index("row")
    loads = [
        pltpu.make_async_copy(src, dst, load_sem.at[k])
        for k, (src, dst) in enumerate((
            (image_ref, ipad.at[HALF : HALF + rows, PAD : PAD + cols]),
            (kernel_hbm, kernel_ref), (gain_hbm, gain_ref), (scale_hbm, scale_ref),
            (cot_hbm, cot_ref), (w_in_hbm, w_in_ref), (w_out_hbm, w_out_ref),
        ))
    ]
    for load in loads:
        load.start()
    has_up = me > 0
    has_dn = me < n - 1

    def signal(target):
        pl.semaphore_signal(
            pltpu.get_barrier_semaphore(), inc=1, device_id={"row": target},
            device_id_type=pl.DeviceIdType.MESH,
        )

    for bit in range(bits):
        signal(other(me, bit))

    @pl.when(has_up)
    def _():
        signal(me - 1)

    @pl.when(has_dn)
    def _():
        signal(me + 1)

    ipad[:, 0:PAD, :] = jnp.zeros((rows + 2 * HALF, PAD, channels), BF)
    ipad[:, PAD + cols :, :] = jnp.zeros((rows + 2 * HALF, PAD, channels), BF)
    edge_rows = jnp.zeros((HALF, cols, channels), BF)
    edge_grad = jnp.zeros(gup.shape, BF)

    @pl.when(me == 0)
    def _():
        ipad[0:HALF, PAD : PAD + cols, :] = edge_rows
        gup[...] = edge_grad

    @pl.when(me == n - 1)
    def _():
        ipad[HALF + rows :, PAD : PAD + cols, :] = edge_rows
        gdn[...] = edge_grad

    count = bits + jnp.where(me > 0, 1, 0) + jnp.where(me < n - 1, 1, 0)
    pl.semaphore_wait(pltpu.get_barrier_semaphore(), count)

    def remote(src, dst, ssem, rsem, target):
        return pltpu.make_async_remote_copy(
            src_ref=src, dst_ref=dst, send_sem=ssem, recv_sem=rsem,
            device_id={"row": target}, device_id_type=pl.DeviceIdType.MESH,
        )

    def halo_dn():
        return remote(image_ref.at[rows - HALF : rows], ipad.at[0:HALF, PAD : PAD + cols],
                      hs.at[0], hr.at[0], me + 1)

    def halo_up():
        return remote(image_ref.at[0:HALF], ipad.at[HALF + rows : rows + 2 * HALF, PAD : PAD + cols],
                      hs.at[1], hr.at[1], me - 1)

    @pl.when(has_dn)
    def _():
        halo_dn().start()

    @pl.when(has_up)
    def _():
        halo_up().start()

    tile = tissue_ref[0, 1]
    flag = tile.astype(F32)
    in_right = jnp.full((1, 1), flag, F32).astype(BF)
    in_left = jnp.full((1, 1), 1.0 - flag, F32).astype(BF)

    def at_tile(ref, r, width):
        left, right = ref[r, 0:width, :], ref[r, TILE_COLS : TILE_COLS + width, :]
        return left * in_left + right * in_right

    loads[1].wait()
    for i in range(KERNEL):
        for j in range(KERNEL):
            tap = kernel_ref[i, j : j + 1, :]
            kf[i * KERNEL + j] = jnp.broadcast_to(tap, (8, channels))
            kb[i * KERNEL + j] = jnp.broadcast_to(tap, (16, channels)).astype(BF)
    for j in range(KERNEL):
        shift_f[:, j * WIN : (j + 1) * WIN] = ones_where((TILE_COLS, WIN), lambda w, x: x == w + j)
        shift_b[j] = ones_where((WIN, TILE_COLS), lambda x, w: x == w + j)
        lanes = slice(j * TILE_COLS, (j + 1) * TILE_COLS)
        low = ones_where((TILE_COLS, TILE_COLS), lambda b, w: w == b - j + HALF)
        right = ones_where((TILE_COLS, TILE_COLS), lambda b, w: w == b - TILE_COLS - j + HALF)
        left = ones_where((TILE_COLS, TILE_COLS), lambda b, w: w == b + TILE_COLS - j + HALF)
        place_m[0:TILE_COLS, lanes] = low
        place_m[TILE_COLS:, lanes] = left
        place_c[0:TILE_COLS, lanes] = right - low
        place_c[TILE_COLS:, lanes] = low - left
    select = ones_where((WIN, WIN + PAD), lambda x, y: y == x + PAD - HALF)
    for load in loads[2:5]:
        load.wait()
    scale = scale_ref[...]
    gain = gain_ref[...]
    for a in range(rows):
        span = slice(a * TILE_COLS, (a + 1) * TILE_COLS)
        upstream = at_tile(cot_ref, a, TILE_COLS).astype(F32)
        grad_ref[span, :] = (scale * upstream).astype(BF)

    def window(r):
        win[r] = mm(select, at_tile(ipad, r, WIN + PAD)).astype(BF)

    loads[0].wait()
    for r in range(HALF, HALF + rows):
        window(r)

    LANES = (slice(0, 128), slice(128, 256))

    def tap(i, j, lanes):
        one = kf[i * KERNEL + j, :, lanes]
        return jnp.concatenate([one, one], axis=0)

    def conv_own(c, _):
        at = pl.ds(pl.multiple_of(c * 16, 16), 16)
        for lanes in LANES:
            lines = [win[HALF + r, at, lanes].astype(F32) for r in range(rows)]
            for j in range(KERNEL):
                taps = [tap(i, j, lanes) for i in range(KERNEL)]
                for a in range(rows):
                    total = lines[0] * taps[HALF - a]
                    for r in range(1, rows):
                        total = total + lines[r] * taps[HALF + r - a]
                    conv_part[a, j, at, lanes] = total
        return 0

    lax.fori_loop(0, WIN // 16, conv_own, 0)

    @pl.when(has_up)
    def _():
        halo_dn().wait_recv()

    for r in range(HALF):
        window(r)

    @pl.when(has_dn)
    def _():
        halo_up().wait_recv()

    for r in range(HALF + rows, rows + 2 * HALF):
        window(r)

    def conv_halo(c, _):
        at = pl.ds(pl.multiple_of(c * 16, 16), 16)
        for lanes in LANES:
            lines = {
                r: win[r, at, lanes].astype(F32)
                for r in range(rows + 2 * HALF) if not HALF <= r < HALF + rows
            }
            for j in range(KERNEL):
                taps = [tap(i, j, lanes) for i in range(KERNEL)]
                for a in range(rows):
                    total = conv_part[a, j, at, lanes]
                    for r in lines:
                        if 0 <= r - a < KERNEL:
                            total = total + lines[r] * taps[r - a]
                    prods[a, j, at, lanes] = total.astype(BF)
        return 0

    lax.fori_loop(0, WIN // 16, conv_halo, 0)

    for a in range(rows):
        span = slice(a * TILE_COLS, (a + 1) * TILE_COLS)
        filtered = mm(shift_f[...], prods[a].reshape(KERNEL * WIN, channels))
        centred = filtered - jnp.mean(filtered, axis=-1, keepdims=True)
        inv_std = lax.rsqrt(jnp.mean(centred * centred, axis=-1, keepdims=True) + EPSILON)
        standard = centred * inv_std
        std_ref[span, :] = standard
        istd_ref[span, :] = inv_std
        normed_ref[span, :] = (standard * gain).astype(BF)

    scat_in = Scatter(me, [0] + list(range(2, bits)) + [1], in_bufs, in_rbufs, in_s, in_r)
    scat_out = Scatter(me, list(range(bits)), out_bufs, out_rbufs, out_s, out_r)
    in_rows = gwin_ref.shape[0]
    out_rows = gwout_ref.shape[0]

    loads[5].wait()
    loads[6].wait()
    normed = normed_ref[...]
    grads = grad_ref[...]
    normed_t = normed.T
    out_parts, in_parts = [], []
    chunks = hidden // FCHUNK

    def forward(f):
        fs = slice(f * FCHUNK, (f + 1) * FCHUNK)
        z_ref[f % 2] = mm(normed, w_in_ref[:, fs])
        back_ref[f % 2] = mm(grads, w_out_ref[fs, :], ((1,), (1,)))

    forward(0)
    for f in range(chunks):
        fs = slice(f * FCHUNK, (f + 1) * FCHUNK)
        if f + 1 < chunks:
            forward(f + 1)
        for m in range(0, positions, BLOCK):
            z = z_ref[f % 2, m : m + BLOCK]
            zz = z * z
            tangent = jnp.tanh(z * (ROOT_TWO_PI + (ROOT_TWO_PI * CUBIC_TERM) * zz))
            half_up = 0.5 + 0.5 * tangent
            value = z * half_up
            slope = half_up + (value * (1.0 - tangent)) * (
                ROOT_TWO_PI + (3.0 * ROOT_TWO_PI * CUBIC_TERM) * zz
            )
            act_ref[m : m + BLOCK, fs] = value.astype(BF)
            pre_ref[m : m + BLOCK, fs] = (back_ref[f % 2, m : m + BLOCK] * slope).astype(BF)
        act = act_ref[:, fs]
        grad_pre = pre_ref[:, fs]
        part = mm(act, grads, ((0,), (0,))).astype(BF)
        per = FCHUNK // out_rows
        for q in range(per):
            out_bufs[0][scat_out.place(f * per + q)] = part[q * out_rows : (q + 1) * out_rows]
        part = mm(normed_t, grad_pre).astype(BF)
        for q in range(n):
            in_bufs[0][scat_in.place(q), :, fs] = part[q * in_rows : (q + 1) * in_rows]
        out_parts.append(scat_out.part(f, (out0_s, out0_r), (pl.ds(f * per // 2, per // 2),)))
        in_parts.append(scat_in.part(f, (in0_s, in0_r), (pl.ds(0, n // 2), slice(None), fs)))
        out_parts[-1].start()
        in_parts[-1].start()

    z_ref[0] = mm(pre_ref[...], w_in_ref[...], ((1,), (1,)))
    gain_sum = jnp.zeros((8, channels), F32)
    for m in range(0, positions, BLOCK):
        span = slice(m, m + BLOCK)
        standard = std_ref[span, :]
        grad_norm = z_ref[0, span]
        grad_std = grad_norm * gain
        both = grad_norm * standard
        mean_g = jnp.mean(grad_std, axis=-1, keepdims=True)
        mean_s = jnp.mean(both * gain, axis=-1, keepdims=True)
        gbuf[16 + m : 16 + m + BLOCK, :] = (
            istd_ref[span, :] * (grad_std - mean_g - standard * mean_s)
        ).astype(BF)
        gain_sum = gain_sum + jnp.sum(both.reshape(BLOCK // 8, 8, channels), axis=0)
    gain_sum = jnp.sum(gain_sum, axis=0, keepdims=True)
    flags = jnp.full((16, channels), flag, F32).astype(BF)
    gbuf[0:16, :] = flags
    gbuf[16 + positions :, :] = flags
    reach = HALF * TILE_COLS

    def grad_up():
        return remote(gbuf.at[0 : 16 + reach], gdn, gs.at[0], gr.at[0], me - 1)

    def grad_dn():
        return remote(gbuf.at[16 + positions - reach : 32 + positions], gup, gs.at[1], gr.at[1], me + 1)

    @pl.when(has_up)
    def _():
        grad_up().start()

    @pl.when(has_dn)
    def _():
        grad_dn().start()

    scat_out.finish_parts(out_parts)
    scat_in.finish_parts(in_parts)

    branch_ref[...] = mm(act_ref[...], w_out_ref[...])
    scale_sum = jnp.zeros((8, channels), F32)
    for a in range(rows):
        upstream = at_tile(cot_ref, a, TILE_COLS).astype(F32)
        both = branch_ref[a * TILE_COLS : (a + 1) * TILE_COLS, :] * upstream
        scale_sum = scale_sum + jnp.sum(both.reshape(TILE_COLS // 8, 8, channels), axis=0)
    scale_sum = jnp.sum(scale_sum, axis=0, keepdims=True)

    for h in range(rows):
        line = gbuf[16 + h * TILE_COLS : 16 + (h + 1) * TILE_COLS, :]
        for j in range(KERNEL):
            gshift[j, h] = mm(shift_b[j], line).astype(BF)
    kacc[...] = jnp.zeros(kacc.shape, F32)

    def kernel_step(c, _):
        at = pl.ds(pl.multiple_of(c * 16, 16), 16)
        lines = [win[r, at, :] for r in range(rows + 2 * HALF)]
        for j in range(KERNEL):
            shifted = [gshift[j, h, at, :] for h in range(rows)]
            for i in range(KERNEL):
                total = lines[i] * shifted[0]
                for h in range(1, rows):
                    total = total + lines[i + h] * shifted[h]
                total = total.astype(F32)
                kacc[i * KERNEL + j] += total[0:8] + total[8:16]
        return 0

    lax.fori_loop(0, WIN // 16, kernel_step, 0)
    for t in range(KERNEL * KERNEL):
        sums[0, t : t + 1, :] = jnp.sum(kacc[t], axis=0, keepdims=True)
    sums[0, 49:50, :] = gain_sum
    sums[0, 50:51, :] = scale_sum
    sums[0, 51:, :] = jnp.zeros((sums.shape[1] - 51, channels), F32)

    def small(k):
        return remote(sums.at[k], sums_in.at[k], sm_s.at[k], sm_r.at[k], other(me, k))

    small(0).start()

    def small_next(k):
        small(k).wait()
        if k + 1 < bits:
            sums[k + 1] = sums[k] + sums_in[k]
            small(k + 1).start()
        else:
            small_ref[...] = (sums[k] + sums_in[k])[: small_ref.shape[0]]

    for a in range(rows):
        for m in range(0, TILE_COLS, BLOCK):
            added = scale * branch_ref[a * TILE_COLS + m : a * TILE_COLS + m + BLOCK, :]
            for s in range(2):
                weight = flag if s == 1 else 1.0 - flag
                at = s * TILE_COLS + m
                base = ipad[HALF + a, PAD + at : PAD + at + BLOCK, :].astype(F32)
                out_ref[a, at : at + BLOCK, :] = (base + weight * added).astype(BF)
    stores[0].start()
    small_next(0)
    scat_out.finish(1, None)
    scat_in.finish(1, None)

    def back_step(c, _):
        at = pl.ds(pl.multiple_of(c * 16, 16), 16)
        own = [gbuf[pl.ds(pl.multiple_of(16 + h * TILE_COLS + c * 16, 16), 16), :] for h in range(rows)]
        for j in range(KERNEL):
            taps = [kb[i * KERNEL + j] for i in range(KERNEL)]
            for a in range(rows):
                total = own[0] * taps[a + HALF]
                for r in range(1, rows):
                    total = total + own[r] * taps[a - r + HALF]
                pown[a, j, at, :] = total
        return 0

    lax.fori_loop(0, TILE_COLS // 16, back_step, 0)

    @pl.when(has_up)
    def _():
        grad_dn().wait_recv()

    @pl.when(has_dn)
    def _():
        grad_up().wait_recv()

    def halo_step(c, _):
        at = pl.ds(pl.multiple_of(c * 16, 16), 16)
        above = [gup[pl.ds(pl.multiple_of(u * TILE_COLS + c * 16, 16), 16), :] for u in range(HALF)]
        below = [gdn[pl.ds(pl.multiple_of(16 + u * TILE_COLS + c * 16, 16), 16), :] for u in range(HALF)]
        for j in range(KERNEL):
            taps = [kb[i * KERNEL + j] for i in range(KERNEL)]
            for a in range(HALF):
                total = above[a] * taps[KERNEL - 1]
                for u in range(a + 1, HALF):
                    total = total + above[u] * taps[a - u + KERNEL - 1]
                pup[a, j, at, :] = total
            for a in range(rows - HALF, rows):
                total = below[0] * taps[a + HALF - rows]
                for v in range(1, a + HALF - rows + 1):
                    total = total + below[v] * taps[a + HALF - rows - v]
                pdn[a - (rows - HALF), j, at, :] = total
        return 0

    lax.fori_loop(0, TILE_COLS // 16, halo_step, 0)
    small_next(1)
    scat_out.finish(2, gwout_ref)
    scat_in.finish(2, gwin_ref)

    def placing(value):
        return place_m[...] + place_c[...] * value

    depth = KERNEL * TILE_COLS
    at_own = placing(in_right)
    at_up = placing(gup[reach : reach + 1, 0:1])
    at_dn = placing(gdn[0:1, 0:1])
    for a in range(rows):
        total = mm(at_own, pown[a].reshape(depth, channels))
        if a < HALF:
            total = total + mm(at_up, pup[a].reshape(depth, channels))
        if a >= rows - HALF:
            total = total + mm(at_dn, pdn[a - (rows - HALF)].reshape(depth, channels))
        gimg_ref[a] = (cot_ref[a].astype(F32) + total).astype(BF)
        if a == 1:
            small_next(2)

    stores[1].start()
    for k in range(3, bits):
        scat_out.finish(k, gwout_ref)
        scat_in.finish(k, gwin_ref)
        small_next(k)
    for store in stores[2:]:
        store.start()

    @pl.when(has_dn)
    def _():
        halo_dn().wait_send()
        grad_dn().wait_send()

    @pl.when(has_up)
    def _():
        halo_up().wait_send()
        grad_up().wait_send()

    for store in stores:
        store.wait()


def copy_out(*refs):
    held, in_sem, out_sem = refs[10:15], refs[15], refs[16]
    reads = [pltpu.make_async_copy(refs[k], held[k], in_sem.at[k]) for k in range(5)]
    writes = [pltpu.make_async_copy(held[k], refs[5 + k], out_sem.at[k]) for k in range(5)]
    for read in reads:
        read.start()
    for read, write in zip(reads, writes):
        read.wait()
        write.start()
    for write in writes:
        write.wait()


def shards(n, image, tissue, kernel, ln_gain, w_in, w_out, layer_scale, cotangent):
    rows, cols, channels = image.shape
    hidden = w_in.shape[1]
    bits = n.bit_length() - 1
    in_rows, out_rows = channels // n, hidden // n
    positions = rows * TILE_COLS
    halo = HALF * TILE_COLS + 16
    vmem = pltpu.VMEM
    outputs = (
        jax.ShapeDtypeStruct((rows, cols, channels), BF),
        jax.ShapeDtypeStruct((rows, cols, channels), BF),
        jax.ShapeDtypeStruct((in_rows, hidden), F32),
        jax.ShapeDtypeStruct((out_rows, channels), F32),
        jax.ShapeDtypeStruct((KERNEL * KERNEL + 2, channels), F32),
    )
    scratch = [
        vmem((2, positions, FCHUNK), F32),
        vmem((2, positions, FCHUNK), F32),
        vmem((positions, hidden), BF),
        vmem((positions, hidden), BF),
        vmem((positions, channels), F32),
        vmem((rows + 2 * HALF, cols + 2 * PAD, channels), BF),
        vmem((rows + 2 * HALF, WIN, channels), BF),
        vmem((KERNEL * KERNEL, 8, channels), F32),
        vmem((KERNEL * KERNEL, 16, channels), BF),
        vmem((TILE_COLS, KERNEL * WIN), BF),
        vmem((2 * TILE_COLS, KERNEL * TILE_COLS), BF),
        vmem((2 * TILE_COLS, KERNEL * TILE_COLS), BF),
        vmem((rows, KERNEL, WIN, channels), BF),
        vmem((positions, channels), BF),
        vmem((positions, channels), F32),
        vmem((positions, 1), F32),
        vmem((positions, channels), BF),
        vmem((positions + 32, channels), BF),
        vmem((halo, channels), BF),
        vmem((halo, channels), BF),
        vmem((KERNEL, rows, WIN, channels), BF),
        vmem((KERNEL * KERNEL, 8, channels), F32),
        vmem((bits, 56, channels), F32),
        vmem((bits, 56, channels), F32),
        vmem((rows, KERNEL, TILE_COLS, channels), BF),
        vmem((HALF, KERNEL, TILE_COLS, channels), BF),
        vmem((HALF, KERNEL, TILE_COLS, channels), BF),
    ]
    for shape in ((in_rows, hidden), (out_rows, channels)):
        scratch += [vmem((n >> k,) + shape, BF) for k in range(bits)]
        scratch += [vmem((n >> (k + 1),) + shape, BF) for k in range(bits)]
    dma = pltpu.SemaphoreType.DMA
    scratch += [dma((2,))] * 4 + [dma((bits,))] * 6
    scratch += [vmem(kernel.shape, F32), vmem((1, channels), F32), vmem(w_in.shape, BF),
                vmem(w_out.shape, BF), vmem((1, channels), F32), vmem(cotangent.shape, BF), dma((7,))]
    scratch += [dma((hidden // FCHUNK,))] * 4
    scratch += [vmem((KERNEL, WIN, TILE_COLS), BF), vmem((rows, KERNEL, WIN, channels), F32)]
    scratch += [vmem(r.shape, r.dtype) for r in outputs] + [dma((5,))]
    anywhere = pl.BlockSpec(memory_space=pl.ANY)
    results = pl.pallas_call(
        functools.partial(body, n, bits),
        out_shape=outputs,
        in_specs=[pl.BlockSpec(memory_space=pltpu.SMEM)] + [anywhere] * 7,
        out_specs=(anywhere,) * 5,
        scratch_shapes=scratch,
        compiler_params=pltpu.CompilerParams(
            collective_id=0, has_side_effects=True, vmem_limit_bytes=60 * 1024 * 1024
        ),
    )(
        tissue, image, kernel, ln_gain.reshape(1, channels), w_in, w_out,
        layer_scale.reshape(1, channels), cotangent,
    )
    return pl.pallas_call(
        copy_out,
        out_shape=[jax.ShapeDtypeStruct(r.shape, r.dtype) for r in results],
        in_specs=[anywhere] * 5,
        out_specs=[anywhere] * 5,
        scratch_shapes=[vmem(r.shape, r.dtype) for r in results] + [dma((5,))] * 2,
        compiler_params=pltpu.CompilerParams(vmem_limit_bytes=60 * 1024 * 1024),
    )(*results)


def solution(mesh):
    placed = (
        P(("group", "row"), None, None),
        P(("group", "row"), None),
        P(),
        P(),
        P(),
        P(),
        P(),
        P(("group", "row"), None, None),
    )
    return jax.shard_map(
        functools.partial(shards, mesh.shape["row"]),
        mesh=mesh,
        in_specs=placed,
        out_specs=(
            P(("group", "row"), None, None),
            P(("group", "row"), None, None),
            P(("group", "row"), None),
            P(("group", "row"), None),
            P("group", None),
        ),
        check_vma=False,
    )
```

```python
import functools

import jax
import jax.numpy as jnp
from jax import lax
from jax.experimental import pallas as pl
from jax.experimental.pallas import tpu as pltpu
from jax.sharding import PartitionSpec as P

KERNEL = 7
HALF = KERNEL // 2
TILE_COLS = 128
PAD = 16
WIN = 144
FCHUNK = 256
BLOCK = 32

EPSILON = 1e-06
ROOT_TWO_PI = 0.7978845608028654
CUBIC_TERM = 0.044715

BF = jnp.bfloat16
F32 = jnp.float32


def ones_where(shape, rule):
    rows = lax.broadcasted_iota(jnp.int32, shape, 0)
    cols = lax.broadcasted_iota(jnp.int32, shape, 1)
    return jnp.where(rule(rows, cols), 1.0, 0.0).astype(BF)


def mm(a, b, dims=((1,), (0,))):
    return lax.dot_general(a, b, (dims, ((), ())), preferred_element_type=F32)


def other(me, bit):
    step = 1 << bit
    return me + step - 2 * step * ((me // step) % 2)


class Scatter:
    def __init__(self, me, order, bufs, rbufs, ssem, rsem):
        self.me, self.order = me, order
        self.bufs, self.rbufs, self.ssem, self.rsem = bufs, rbufs, ssem, rsem

    def place(self, chunk):
        return (chunk % 2) * self.rbufs[0].shape[0] + chunk // 2

    def place_next(self, chunk):
        n = len(self.order)
        return sum(((chunk >> bit) & 1) << (n - 1 - k) for k, bit in enumerate(self.order) if k)

    def halves(self, k):
        half = self.rbufs[k].shape[0]
        mine = (self.me // (1 << self.order[k])) % 2
        return half, mine

    def copy(self, k):
        half, mine = self.halves(k)
        return pltpu.make_async_remote_copy(
            src_ref=self.bufs[k].at[pl.ds((1 - mine) * half, half)],
            dst_ref=self.rbufs[k],
            send_sem=self.ssem.at[k],
            recv_sem=self.rsem.at[k],
            device_id={"row": other(self.me, self.order[k])},
            device_id_type=pl.DeviceIdType.MESH,
        )

    def start(self, k):
        self.copy(k).start()

    def part(self, index, sems, picks):
        half, mine = self.halves(0)
        first, *rest = picks
        return pltpu.make_async_remote_copy(
            src_ref=self.bufs[0].at[(pl.ds((1 - mine) * half + first.start, first.size), *rest)],
            dst_ref=self.rbufs[0].at[(first, *rest)],
            send_sem=sems[0].at[index],
            recv_sem=sems[1].at[index],
            device_id={"row": other(self.me, self.order[0])},
            device_id_type=pl.DeviceIdType.MESH,
        )

    def finish_parts(self, parts):
        for part in parts:
            part.wait()
        half, mine = self.halves(0)
        for e in range(half):
            self.bufs[1][self.place_next(2 * e)] = self.bufs[0][mine * half + e] + self.rbufs[0][e]
        self.start(1)

    def finish(self, k, out_ref):
        self.copy(k).wait()
        half, mine = self.halves(k)
        if k + 1 < len(self.order):
            def step(c, _):
                self.bufs[k + 1][c] = self.bufs[k][mine * half + c] + self.rbufs[k][c]
                return 0

            lax.fori_loop(0, half, step, 0)
            self.start(k + 1)
        else:
            out_ref[...] = self.bufs[k][mine].astype(F32) + self.rbufs[k][0].astype(F32)


def body(
    n, bits,
    tissue_ref, image_ref, kernel_hbm, gain_hbm, w_in_hbm, w_out_hbm, scale_hbm, cot_hbm,
    out_hbm, gimg_hbm, gwin_hbm, gwout_hbm, small_hbm,
    *scratch,
):
    (z_ref, back_ref, act_ref, pre_ref, branch_ref, ipad, win, kf, kb, shift_f, place_m, place_c, prods, normed_ref, std_ref, istd_ref, grad_ref,
     gbuf, gup, gdn, gshift, kacc, sums, sums_in, pown, pup, pdn) = scratch[:27]
    in_bufs = scratch[27 : 27 + bits]
    in_rbufs = scratch[27 + bits : 27 + 2 * bits]
    out_bufs = scratch[27 + 2 * bits : 27 + 3 * bits]
    out_rbufs = scratch[27 + 3 * bits : 27 + 4 * bits]
    (hs, hr, gs, gr, in_s, in_r, out_s, out_r, sm_s, sm_r) = scratch[27 + 4 * bits : 27 + 4 * bits + 10]

    kernel_ref, gain_ref, w_in_ref, w_out_ref, scale_ref, cot_ref, load_sem = scratch[27 + 4 * bits + 10 : -17]
    out_ref, gimg_ref, gwin_ref, gwout_ref, small_ref, store_sem = scratch[-6:]
    (in0_s, in0_r, out0_s, out0_r, flag_out, flag_in, halo_out, flag_s, flag_r,
     shift_b, conv_part) = scratch[-17:-6]
    stores = [
        pltpu.make_async_copy(src, dst, store_sem.at[k])
        for k, (src, dst) in enumerate((
            (out_ref, out_hbm), (gimg_ref, gimg_hbm), (gwin_ref, gwin_hbm),
            (gwout_ref, gwout_hbm), (small_ref, small_hbm),
        ))
    ]
    rows, cols, channels = image_ref.shape
    hidden = w_in_ref.shape[1]
    positions = rows * TILE_COLS
    me = lax.axis_index("row")
    loads = [
        pltpu.make_async_copy(src, dst, load_sem.at[k])
        for k, (src, dst) in enumerate((
            (image_ref, ipad.at[:, PAD : PAD + cols]),
            (kernel_hbm, kernel_ref), (gain_hbm, gain_ref), (scale_hbm, scale_ref),
            (cot_hbm, cot_ref), (w_in_hbm, w_in_ref), (w_out_hbm, w_out_ref),
        ))
    ]
    for load in loads:
        load.start()
    has_up = me > 0
    has_dn = me < n - 1

    def signal(target):
        pl.semaphore_signal(
            pltpu.get_barrier_semaphore(), inc=1, device_id={"row": target},
            device_id_type=pl.DeviceIdType.MESH,
        )

    for bit in range(bits):
        signal(other(me, bit))

    @pl.when(has_up)
    def _():
        signal(me - 1)

    @pl.when(has_dn)
    def _():
        signal(me + 1)

    tile = tissue_ref[0, 1]
    flag = tile.astype(F32)
    flag_out[...] = jnp.full(flag_out.shape, flag, F32)
    ipad[:, 0:PAD, :] = jnp.zeros((rows, PAD, channels), BF)
    ipad[:, PAD + cols :, :] = jnp.zeros((rows, PAD, channels), BF)
    edge_rows = jnp.zeros((HALF, WIN, channels), BF)
    edge_grad = jnp.zeros(gup.shape, BF)
    edge_flag = jnp.zeros(flag_out.shape, F32)

    @pl.when(me == 0)
    def _():
        win[0:HALF] = edge_rows
        gup[...] = edge_grad
        flag_in[0] = edge_flag

    @pl.when(me == n - 1)
    def _():
        win[HALF + rows :] = edge_rows
        gdn[...] = edge_grad
        flag_in[1] = edge_flag

    count = bits + jnp.where(me > 0, 1, 0) + jnp.where(me < n - 1, 1, 0)
    pl.semaphore_wait(pltpu.get_barrier_semaphore(), count)

    def remote(src, dst, ssem, rsem, target):
        return pltpu.make_async_remote_copy(
            src_ref=src, dst_ref=dst, send_sem=ssem, recv_sem=rsem,
            device_id={"row": target}, device_id_type=pl.DeviceIdType.MESH,
        )

    def flag_dn():
        return remote(flag_out, flag_in.at[0], flag_s.at[0], flag_r.at[0], me + 1)

    def flag_up():
        return remote(flag_out, flag_in.at[1], flag_s.at[1], flag_r.at[1], me - 1)

    def halo_dn():
        return remote(halo_out.at[0], win.at[0:HALF], hs.at[0], hr.at[0], me + 1)

    def halo_up():
        return remote(halo_out.at[1], win.at[HALF + rows : rows + 2 * HALF], hs.at[1], hr.at[1], me - 1)

    @pl.when(has_dn)
    def _():
        flag_dn().start()

    @pl.when(has_up)
    def _():
        flag_up().start()

    select = ones_where((WIN, WIN + PAD), lambda x, y: y == x + PAD - HALF)

    def at_tile(ref, r, width, value):
        left, right = ref[r, 0:width, :], ref[r, TILE_COLS : TILE_COLS + width, :]
        right_part = value.astype(BF)
        return left * (1.0 - value).astype(BF) + right * right_part

    def window(r, value):
        return mm(select, at_tile(ipad, r, WIN + PAD, value)).astype(BF)

    in_right = jnp.full((1, 1), flag, F32)
    loads[0].wait()

    @pl.when(has_dn)
    def _():
        flag_up().wait_recv()

    for r in range(HALF):
        halo_out[0, r] = window(rows - HALF + r, flag_in[1, 0:1, 0:1])

    @pl.when(has_dn)
    def _():
        halo_dn().start()

    @pl.when(has_up)
    def _():
        flag_dn().wait_recv()

    for r in range(HALF):
        halo_out[1, r] = window(r, flag_in[0, 0:1, 0:1])

    @pl.when(has_up)
    def _():
        halo_up().start()

    for r in range(rows):
        win[HALF + r] = window(r, in_right)

    loads[1].wait()
    for i in range(KERNEL):
        for j in range(KERNEL):
            tap = kernel_ref[i, j : j + 1, :]
            kf[i * KERNEL + j] = jnp.broadcast_to(tap, (8, channels))
            kb[i * KERNEL + j] = jnp.broadcast_to(tap, (16, channels)).astype(BF)
    for j in range(KERNEL):
        shift_f[:, j * WIN : (j + 1) * WIN] = ones_where((TILE_COLS, WIN), lambda w, x: x == w + j)
        shift_b[j] = ones_where((WIN, TILE_COLS), lambda x, w: x == w + j)
        lanes = slice(j * TILE_COLS, (j + 1) * TILE_COLS)
        low = ones_where((TILE_COLS, TILE_COLS), lambda b, w: w == b - j + HALF)
        right = ones_where((TILE_COLS, TILE_COLS), lambda b, w: w == b - TILE_COLS - j + HALF)
        left = ones_where((TILE_COLS, TILE_COLS), lambda b, w: w == b + TILE_COLS - j + HALF)
        place_m[0:TILE_COLS, lanes] = low
        place_m[TILE_COLS:, lanes] = left
        place_c[0:TILE_COLS, lanes] = right - low
        place_c[TILE_COLS:, lanes] = low - left
    for load in loads[2:5]:
        load.wait()
    scale = scale_ref[...]
    gain = gain_ref[...]
    for a in range(rows):
        span = slice(a * TILE_COLS, (a + 1) * TILE_COLS)
        upstream = at_tile(cot_ref, a, TILE_COLS, in_right).astype(F32)
        grad_ref[span, :] = (scale * upstream).astype(BF)

    LANES = (slice(0, 128), slice(128, 256))

    def tap(i, j, lanes):
        one = kf[i * KERNEL + j, :, lanes]
        return jnp.concatenate([one, one], axis=0)

    def conv_own(c, _):
        at = pl.ds(pl.multiple_of(c * 16, 16), 16)
        for lanes in LANES:
            lines = [win[HALF + r, at, lanes].astype(F32) for r in range(rows)]
            for j in range(KERNEL):
                taps = [tap(i, j, lanes) for i in range(KERNEL)]
                for a in range(rows):
                    total = lines[0] * taps[HALF - a]
                    for r in range(1, rows):
                        total = total + lines[r] * taps[HALF + r - a]
                    conv_part[a, j, at, lanes] = total
        return 0

    lax.fori_loop(0, WIN // 16, conv_own, 0)

    @pl.when(has_up)
    def _():
        halo_dn().wait_recv()

    @pl.when(has_dn)
    def _():
        halo_up().wait_recv()

    def conv_halo(c, _):
        at = pl.ds(pl.multiple_of(c * 16, 16), 16)
        for lanes in LANES:
            lines = {
                r: win[r, at, lanes].astype(F32)
                for r in range(rows + 2 * HALF) if not HALF <= r < HALF + rows
            }
            for j in range(KERNEL):
                taps = [tap(i, j, lanes) for i in range(KERNEL)]
                for a in range(rows):
                    total = conv_part[a, j, at, lanes]
                    for r in lines:
                        if 0 <= r - a < KERNEL:
                            total = total + lines[r] * taps[r - a]
                    prods[a, j, at, lanes] = total.astype(BF)
        return 0

    lax.fori_loop(0, WIN // 16, conv_halo, 0)

    for a in range(rows):
        span = slice(a * TILE_COLS, (a + 1) * TILE_COLS)
        filtered = mm(shift_f[...], prods[a].reshape(KERNEL * WIN, channels))
        centred = filtered - jnp.mean(filtered, axis=-1, keepdims=True)
        inv_std = lax.rsqrt(jnp.mean(centred * centred, axis=-1, keepdims=True) + EPSILON)
        standard = centred * inv_std
        std_ref[span, :] = standard
        istd_ref[span, :] = inv_std
        normed_ref[span, :] = (standard * gain).astype(BF)

    scat_in = Scatter(me, [0] + list(range(2, bits)) + [1], in_bufs, in_rbufs, in_s, in_r)
    scat_out = Scatter(me, list(range(bits)), out_bufs, out_rbufs, out_s, out_r)
    in_rows = gwin_ref.shape[0]
    out_rows = gwout_ref.shape[0]

    loads[5].wait()
    loads[6].wait()
    normed = normed_ref[...]
    grads = grad_ref[...]
    normed_t = normed.T
    out_parts, in_parts = [], []
    chunks = hidden // FCHUNK

    def forward(f):
        fs = slice(f * FCHUNK, (f + 1) * FCHUNK)
        z_ref[f % 2] = mm(normed, w_in_ref[:, fs])
        back_ref[f % 2] = mm(grads, w_out_ref[fs, :], ((1,), (1,)))

    forward(0)
    for f in range(chunks):
        fs = slice(f * FCHUNK, (f + 1) * FCHUNK)
        if f + 1 < chunks:
            forward(f + 1)
        for m in range(0, positions, BLOCK):
            z = z_ref[f % 2, m : m + BLOCK]
            zz = z * z
            tangent = jnp.tanh(z * (ROOT_TWO_PI + (ROOT_TWO_PI * CUBIC_TERM) * zz))
            half_up = 0.5 + 0.5 * tangent
            value = z * half_up
            slope = half_up + (value * (1.0 - tangent)) * (
                ROOT_TWO_PI + (3.0 * ROOT_TWO_PI * CUBIC_TERM) * zz
            )
            act_ref[m : m + BLOCK, fs] = value.astype(BF)
            pre_ref[m : m + BLOCK, fs] = (back_ref[f % 2, m : m + BLOCK] * slope).astype(BF)
        act = act_ref[:, fs]
        grad_pre = pre_ref[:, fs]
        part = mm(act, grads, ((0,), (0,))).astype(BF)
        per = FCHUNK // out_rows
        for q in range(per):
            out_bufs[0][scat_out.place(f * per + q)] = part[q * out_rows : (q + 1) * out_rows]
        part = mm(normed_t, grad_pre).astype(BF)
        for q in range(n):
            in_bufs[0][scat_in.place(q), :, fs] = part[q * in_rows : (q + 1) * in_rows]
        out_parts.append(scat_out.part(f, (out0_s, out0_r), (pl.ds(f * per // 2, per // 2),)))
        in_parts.append(scat_in.part(f, (in0_s, in0_r), (pl.ds(0, n // 2), slice(None), fs)))
        out_parts[-1].start()
        in_parts[-1].start()

    z_ref[0] = mm(pre_ref[...], w_in_ref[...], ((1,), (1,)))
    gain_sum = jnp.zeros((8, channels), F32)
    for m in range(0, positions, BLOCK):
        span = slice(m, m + BLOCK)
        standard = std_ref[span, :]
        grad_norm = z_ref[0, span]
        grad_std = grad_norm * gain
        both = grad_norm * standard
        mean_g = jnp.mean(grad_std, axis=-1, keepdims=True)
        mean_s = jnp.mean(both * gain, axis=-1, keepdims=True)
        gbuf[16 + m : 16 + m + BLOCK, :] = (
            istd_ref[span, :] * (grad_std - mean_g - standard * mean_s)
        ).astype(BF)
        gain_sum = gain_sum + jnp.sum(both.reshape(BLOCK // 8, 8, channels), axis=0)
    gain_sum = jnp.sum(gain_sum, axis=0, keepdims=True)
    flags = jnp.full((16, channels), flag, F32).astype(BF)
    gbuf[0:16, :] = flags
    gbuf[16 + positions :, :] = flags
    reach = HALF * TILE_COLS

    def grad_up():
        return remote(gbuf.at[0 : 16 + reach], gdn, gs.at[0], gr.at[0], me - 1)

    def grad_dn():
        return remote(gbuf.at[16 + positions - reach : 32 + positions], gup, gs.at[1], gr.at[1], me + 1)

    @pl.when(has_up)
    def _():
        grad_up().start()

    @pl.when(has_dn)
    def _():
        grad_dn().start()

    scat_out.finish_parts(out_parts)
    scat_in.finish_parts(in_parts)

    branch_ref[...] = mm(act_ref[...], w_out_ref[...])
    scale_sum = jnp.zeros((8, channels), F32)
    for a in range(rows):
        upstream = at_tile(cot_ref, a, TILE_COLS, in_right).astype(F32)
        both = branch_ref[a * TILE_COLS : (a + 1) * TILE_COLS, :] * upstream
        scale_sum = scale_sum + jnp.sum(both.reshape(TILE_COLS // 8, 8, channels), axis=0)
    scale_sum = jnp.sum(scale_sum, axis=0, keepdims=True)

    for h in range(rows):
        line = gbuf[16 + h * TILE_COLS : 16 + (h + 1) * TILE_COLS, :]
        for j in range(KERNEL):
            gshift[j, h] = mm(shift_b[j], line).astype(BF)
    kacc[...] = jnp.zeros(kacc.shape, F32)

    def kernel_step(c, _):
        at = pl.ds(pl.multiple_of(c * 16, 16), 16)
        lines = [win[r, at, :] for r in range(rows + 2 * HALF)]
        for j in range(KERNEL):
            shifted = [gshift[j, h, at, :] for h in range(rows)]
            for i in range(KERNEL):
                total = lines[i] * shifted[0]
                for h in range(1, rows):
                    total = total + lines[i + h] * shifted[h]
                total = total.astype(F32)
                kacc[i * KERNEL + j] += total[0:8] + total[8:16]
        return 0

    lax.fori_loop(0, WIN // 16, kernel_step, 0)
    for t in range(KERNEL * KERNEL):
        sums[0, t : t + 1, :] = jnp.sum(kacc[t], axis=0, keepdims=True)
    sums[0, 49:50, :] = gain_sum
    sums[0, 50:51, :] = scale_sum
    sums[0, 51:, :] = jnp.zeros((sums.shape[1] - 51, channels), F32)

    def small(k):
        return remote(sums.at[k], sums_in.at[k], sm_s.at[k], sm_r.at[k], other(me, k))

    small(0).start()

    def small_next(k):
        small(k).wait()
        if k + 1 < bits:
            sums[k + 1] = sums[k] + sums_in[k]
            small(k + 1).start()
        else:
            small_ref[...] = (sums[k] + sums_in[k])[: small_ref.shape[0]]

    for a in range(rows):
        for m in range(0, TILE_COLS, BLOCK):
            added = scale * branch_ref[a * TILE_COLS + m : a * TILE_COLS + m + BLOCK, :]
            for s in range(2):
                weight = flag if s == 1 else 1.0 - flag
                at = s * TILE_COLS + m
                base = ipad[a, PAD + at : PAD + at + BLOCK, :].astype(F32)
                out_ref[a, at : at + BLOCK, :] = (base + weight * added).astype(BF)
    stores[0].start()
    small_next(0)
    scat_out.finish(1, None)
    scat_in.finish(1, None)

    def back_step(c, _):
        at = pl.ds(pl.multiple_of(c * 16, 16), 16)
        own = [gbuf[pl.ds(pl.multiple_of(16 + h * TILE_COLS + c * 16, 16), 16), :] for h in range(rows)]
        for j in range(KERNEL):
            taps = [kb[i * KERNEL + j] for i in range(KERNEL)]
            for a in range(rows):
                total = own[0] * taps[a + HALF]
                for r in range(1, rows):
                    total = total + own[r] * taps[a - r + HALF]
                pown[a, j, at, :] = total
        return 0

    lax.fori_loop(0, TILE_COLS // 16, back_step, 0)

    @pl.when(has_up)
    def _():
        grad_dn().wait_recv()

    @pl.when(has_dn)
    def _():
        grad_up().wait_recv()

    def halo_step(c, _):
        at = pl.ds(pl.multiple_of(c * 16, 16), 16)
        above = [gup[pl.ds(pl.multiple_of(u * TILE_COLS + c * 16, 16), 16), :] for u in range(HALF)]
        below = [gdn[pl.ds(pl.multiple_of(16 + u * TILE_COLS + c * 16, 16), 16), :] for u in range(HALF)]
        for j in range(KERNEL):
            taps = [kb[i * KERNEL + j] for i in range(KERNEL)]
            for a in range(HALF):
                total = above[a] * taps[KERNEL - 1]
                for u in range(a + 1, HALF):
                    total = total + above[u] * taps[a - u + KERNEL - 1]
                pup[a, j, at, :] = total
            for a in range(rows - HALF, rows):
                total = below[0] * taps[a + HALF - rows]
                for v in range(1, a + HALF - rows + 1):
                    total = total + below[v] * taps[a + HALF - rows - v]
                pdn[a - (rows - HALF), j, at, :] = total
        return 0

    lax.fori_loop(0, TILE_COLS // 16, halo_step, 0)
    small_next(1)
    scat_out.finish(2, gwout_ref)
    scat_in.finish(2, gwin_ref)

    def placing(value):
        return place_m[...] + place_c[...] * value

    depth = KERNEL * TILE_COLS
    at_own = placing(in_right.astype(BF))
    at_up = placing(gup[reach : reach + 1, 0:1])
    at_dn = placing(gdn[0:1, 0:1])
    for a in range(rows):
        total = mm(at_own, pown[a].reshape(depth, channels))
        if a < HALF:
            total = total + mm(at_up, pup[a].reshape(depth, channels))
        if a >= rows - HALF:
            total = total + mm(at_dn, pdn[a - (rows - HALF)].reshape(depth, channels))
        gimg_ref[a] = (cot_ref[a].astype(F32) + total).astype(BF)
        if a == 1:
            small_next(2)

    stores[1].start()
    for k in range(3, bits):
        scat_out.finish(k, gwout_ref)
        scat_in.finish(k, gwin_ref)
        small_next(k)
    for store in stores[2:]:
        store.start()

    @pl.when(has_dn)
    def _():
        flag_dn().wait_send()
        halo_dn().wait_send()
        grad_dn().wait_send()

    @pl.when(has_up)
    def _():
        flag_up().wait_send()
        halo_up().wait_send()
        grad_up().wait_send()

    for store in stores:
        store.wait()


def copy_out(*refs):
    held, in_sem, out_sem = refs[10:15], refs[15], refs[16]
    reads = [pltpu.make_async_copy(refs[k], held[k], in_sem.at[k]) for k in range(5)]
    writes = [pltpu.make_async_copy(held[k], refs[5 + k], out_sem.at[k]) for k in range(5)]
    for read in reads:
        read.start()
    for read, write in zip(reads, writes):
        read.wait()
        write.start()
    for write in writes:
        write.wait()


def shards(n, image, tissue, kernel, ln_gain, w_in, w_out, layer_scale, cotangent):
    rows, cols, channels = image.shape
    hidden = w_in.shape[1]
    bits = n.bit_length() - 1
    in_rows, out_rows = channels // n, hidden // n
    positions = rows * TILE_COLS
    halo = HALF * TILE_COLS + 16
    vmem = pltpu.VMEM
    outputs = (
        jax.ShapeDtypeStruct((rows, cols, channels), BF),
        jax.ShapeDtypeStruct((rows, cols, channels), BF),
        jax.ShapeDtypeStruct((in_rows, hidden), F32),
        jax.ShapeDtypeStruct((out_rows, channels), F32),
        jax.ShapeDtypeStruct((KERNEL * KERNEL + 2, channels), F32),
    )
    scratch = [
        vmem((2, positions, FCHUNK), F32),
        vmem((2, positions, FCHUNK), F32),
        vmem((positions, hidden), BF),
        vmem((positions, hidden), BF),
        vmem((positions, channels), F32),
        vmem((rows, cols + 2 * PAD, channels), BF),
        vmem((rows + 2 * HALF, WIN, channels), BF),
        vmem((KERNEL * KERNEL, 8, channels), F32),
        vmem((KERNEL * KERNEL, 16, channels), BF),
        vmem((TILE_COLS, KERNEL * WIN), BF),
        vmem((2 * TILE_COLS, KERNEL * TILE_COLS), BF),
        vmem((2 * TILE_COLS, KERNEL * TILE_COLS), BF),
        vmem((rows, KERNEL, WIN, channels), BF),
        vmem((positions, channels), BF),
        vmem((positions, channels), F32),
        vmem((positions, 1), F32),
        vmem((positions, channels), BF),
        vmem((positions + 32, channels), BF),
        vmem((halo, channels), BF),
        vmem((halo, channels), BF),
        vmem((KERNEL, rows, WIN, channels), BF),
        vmem((KERNEL * KERNEL, 8, channels), F32),
        vmem((bits, 56, channels), F32),
        vmem((bits, 56, channels), F32),
        vmem((rows, KERNEL, TILE_COLS, channels), BF),
        vmem((HALF, KERNEL, TILE_COLS, channels), BF),
        vmem((HALF, KERNEL, TILE_COLS, channels), BF),
    ]
    for shape in ((in_rows, hidden), (out_rows, channels)):
        scratch += [vmem((n >> k,) + shape, BF) for k in range(bits)]
        scratch += [vmem((n >> (k + 1),) + shape, BF) for k in range(bits)]
    dma = pltpu.SemaphoreType.DMA
    scratch += [dma((2,))] * 4 + [dma((bits,))] * 6
    scratch += [vmem(kernel.shape, F32), vmem((1, channels), F32), vmem(w_in.shape, BF),
                vmem(w_out.shape, BF), vmem((1, channels), F32), vmem(cotangent.shape, BF), dma((7,))]
    scratch += [dma((hidden // FCHUNK,))] * 4
    scratch += [vmem((8, 128), F32), vmem((2, 8, 128), F32), vmem((2, HALF, WIN, channels), BF)]
    scratch += [dma((2,))] * 2
    scratch += [vmem((KERNEL, WIN, TILE_COLS), BF), vmem((rows, KERNEL, WIN, channels), F32)]
    scratch += [vmem(r.shape, r.dtype) for r in outputs] + [dma((5,))]
    anywhere = pl.BlockSpec(memory_space=pl.ANY)
    results = pl.pallas_call(
        functools.partial(body, n, bits),
        out_shape=outputs,
        in_specs=[pl.BlockSpec(memory_space=pltpu.SMEM)] + [anywhere] * 7,
        out_specs=(anywhere,) * 5,
        scratch_shapes=scratch,
        compiler_params=pltpu.CompilerParams(
            collective_id=0, has_side_effects=True, vmem_limit_bytes=60 * 1024 * 1024
        ),
    )(
        tissue, image, kernel, ln_gain.reshape(1, channels), w_in, w_out,
        layer_scale.reshape(1, channels), cotangent,
    )
    return pl.pallas_call(
        copy_out,
        out_shape=[jax.ShapeDtypeStruct(r.shape, r.dtype) for r in results],
        in_specs=[anywhere] * 5,
        out_specs=[anywhere] * 5,
        scratch_shapes=[vmem(r.shape, r.dtype) for r in results] + [dma((5,))] * 2,
        compiler_params=pltpu.CompilerParams(vmem_limit_bytes=60 * 1024 * 1024),
    )(*results)


def solution(mesh):
    placed = (
        P(("group", "row"), None, None),
        P(("group", "row"), None),
        P(),
        P(),
        P(),
        P(),
        P(),
        P(("group", "row"), None, None),
    )
    return jax.shard_map(
        functools.partial(shards, mesh.shape["row"]),
        mesh=mesh,
        in_specs=placed,
        out_specs=(
            P(("group", "row"), None, None),
            P(("group", "row"), None, None),
            P(("group", "row"), None),
            P(("group", "row"), None),
            P("group", None),
        ),
        check_vma=False,
    )
```
